256 devices in a mesh: ctx: 64 (over z, y, core), batch: 4 (over x).
Axes of the slice: x: 4, y: 4, z: 8, core: 2. Of those that a mesh axis runs over, the one named last changes fastest.
Arguments:
- queries: bfloat16 [2048, 2, 8192], P(('ctx', 'batch')), may hold values from -40 to 40
- new_keys: bfloat16 [2048, 2, 1024], P(('ctx', 'batch')), may hold values from -18 to 18
- new_values: bfloat16 [2048, 2, 1024], P(('ctx', 'batch')), may hold values from -6 to 6
- suffix_keys: bfloat16 [2048, 32, 1024], P(('ctx', 'batch')), may hold values from -15 to 15
- suffix_values: bfloat16 [2048, 32, 1024], P(('ctx', 'batch')), may hold values from -6 to 6
- suffix_length: int32 [2048], P(('ctx', 'batch')), may hold values from 1 to 32
- group_ids: int32 [2048, 1], P('ctx'), may hold values from 0 to 63, as said below
- prefix_keys: bfloat16 [64, 256, 1024], P('ctx', None, 'batch'), may hold values from -6 to 6
- prefix_values: bfloat16 [64, 256, 1024], P('ctx', None, 'batch'), may hold values from -6 to 6
- prefix_length: int32 [64], P('ctx'), may hold values from 64 to 256
Outputs:
- attended: bfloat16 [2048, 2, 8192], P(('ctx', 'batch'))
The draws below stay inside these ranges and needn't reach their ends.
Inputs may be any that keep to these rules, and one draw needn't show every extreme that they name: `group_ids`: in each aligned block of 32 rows no group is named more than 2 times, and some group is named exactly 2 times in every block.
All inputs are finite; a program needn't handle non-finite values.
Results may differ from the reference program's by a relative error of at most 0.0026.
Values may be sent and summed in bfloat16 or wider, within the bound.
No kernel may reach another device: no remote copies, remote signals or barrier semaphores. Data moves between devices by JAX's collectives and lax.ppermute only.
A program may use at most 128 MiB of HBM per device.

```python
import math
import jax
import jax.numpy as jnp
from jax import lax

HEADS = 64
KV_HEADS = 8
HEAD_DIM = 128
PREFIX_MAX = 256
STEPS = 2
SUFFIX_MAX = 32
GROUPS = 64
BLOCK_ROWS = 32
CAPACITY = 2
REQUESTS = 2048


def route_rows(key):
    key = jax.random.fold_in(key, 5)
    first_key, second_key = jax.random.split(key)
    popular = jax.random.randint(first_key, (), 0, GROUPS, dtype=jnp.int32)
    others = (popular + 1 + jnp.arange(GROUPS - 1, dtype=jnp.int32)) % GROUPS
    candidates = jnp.tile(others, CAPACITY)

    def one_block(block_key):
        left_key, right_key = jax.random.split(block_key)
        chosen = jax.random.permutation(left_key, candidates)[:BLOCK_ROWS - CAPACITY]
        filled = jnp.concatenate([chosen, jnp.full((CAPACITY,), popular, jnp.int32)])
        return jax.random.permutation(right_key, filled)
    block_keys = jax.random.split(second_key, REQUESTS // BLOCK_ROWS)
    return jax.vmap(one_block)(block_keys).reshape(REQUESTS, 1).astype(jnp.int32)


def draw_group_ids(key, part):
    return route_rows(key)


def draw_queries(key, part):
    key = jax.random.fold_in(key, 11)
    full_shape = (REQUESTS, STEPS, HEADS * HEAD_DIM)
    return jax.random.truncated_normal(key, -6.0, 6.0, full_shape).astype(jnp.bfloat16)


def draw_new_keys(key, part):
    key = jax.random.fold_in(key, 12)
    full_shape = (REQUESTS, STEPS, KV_HEADS * HEAD_DIM)
    return (3.0 * jax.random.truncated_normal(key, -6.0, 6.0, full_shape)).astype(jnp.bfloat16)


def draw_prefix_keys(key, part):
    key = jax.random.fold_in(key, 14)
    full_shape = (GROUPS, PREFIX_MAX, KV_HEADS * HEAD_DIM)
    return jax.random.truncated_normal(key, -6.0, 6.0, full_shape).astype(jnp.bfloat16)


def draw_prefix_length(key, part):
    key = jax.random.fold_in(key, 21)
    first_key, second_key = jax.random.split(key)
    lengths = jax.random.randint(first_key, (GROUPS,), PREFIX_MAX // 4, PREFIX_MAX + 1, dtype=jnp.int32)
    longest = jax.random.randint(second_key, (), 0, GROUPS, dtype=jnp.int32)
    return lengths.at[longest].set(PREFIX_MAX)


def draw_suffix_length(key, part):
    key = jax.random.fold_in(key, 22)
    first_key, second_key = jax.random.split(key)
    lengths = jax.random.randint(first_key, (REQUESTS,), 1, SUFFIX_MAX + 1, dtype=jnp.int32)
    longest = jax.random.randint(second_key, (), 0, REQUESTS, dtype=jnp.int32)
    return lengths.at[longest].set(SUFFIX_MAX)


def block_levels(key, dims, shards, low, high):
    gain = 1.0
    for dim, parts in shards:
        heights = jax.random.uniform(jax.random.fold_in(jax.random.fold_in(key, 6), dim), (parts,), jnp.float32, low / len(shards), high / len(shards))
        gain = gain * jnp.repeat(jnp.exp(heights), dims[dim] // parts).reshape((-1,) + (1,) * (len(dims) - 1 - dim))
    return gain


def bell_draw(own_key, shape, width, bound, pieces=(), kind=jnp.bfloat16):
    values = width * jax.random.normal(own_key, shape, jnp.float32)
    if pieces:
        values = values * block_levels(own_key, shape, pieces, -0.22, 0.18)
    return jnp.clip(values, -bound, bound).astype(kind)


def setup_inputs(seed: int = 0) -> dict:
    keys = jax.random.split(jax.random.key(seed), 11)
    queries = draw_queries(jax.random.fold_in(keys[10], 71), 0)
    new_keys = draw_new_keys(jax.random.fold_in(keys[10], 71), 0)
    new_values = bell_draw(keys[2], (REQUESTS, STEPS, KV_HEADS * HEAD_DIM), 1.0, 6.0, ((0, 256),))
    suffix_keys = bell_draw(keys[3], (REQUESTS, SUFFIX_MAX, KV_HEADS * HEAD_DIM), 2.5, 15.0, ((0, 256),))
    suffix_values = bell_draw(keys[4], (REQUESTS, SUFFIX_MAX, KV_HEADS * HEAD_DIM), 1.0, 6.0, ((0, 256),))
    suffix_length = draw_suffix_length(jax.random.fold_in(keys[10], 71), 0)
    group_ids = draw_group_ids(jax.random.fold_in(keys[10], 71), 0)
    prefix_keys = draw_prefix_keys(jax.random.fold_in(keys[10], 71), 0)
    prefix_values = bell_draw(keys[8], (GROUPS, PREFIX_MAX, KV_HEADS * HEAD_DIM), 1.0, 6.0, ((0, 64), (2, 4)))
    prefix_length = draw_prefix_length(jax.random.fold_in(keys[10], 71), 0)
    return {"queries": queries, "new_keys": new_keys, "new_values": new_values, "suffix_keys": suffix_keys, "suffix_values": suffix_values, "suffix_length": suffix_length, "group_ids": group_ids, "prefix_keys": prefix_keys, "prefix_values": prefix_values, "prefix_length": prefix_length}


def partial_softmax(scores, usable):
    highest = lax.optimization_barrier(jnp.max(jnp.where(usable, scores, -jnp.inf), axis=-1))
    weights = jnp.where(usable, jnp.exp(scores - highest[..., None]), 0.0)
    return (highest, weights, lax.optimization_barrier(jnp.sum(weights, axis=-1)))

def reference(queries, new_keys, new_values, suffix_keys, suffix_values, suffix_length, group_ids, prefix_keys, prefix_values, prefix_length):
    group_size = HEADS // KV_HEADS
    factor = 1.0 / math.sqrt(HEAD_DIM)
    group_of = group_ids[:, 0].astype(jnp.int32)

    def one_request(request):
        query, fresh_keys, fresh_values, own_keys, own_values, own_length, group = request
        query_rows = query.astype(jnp.float32).reshape(STEPS, KV_HEADS, group_size, HEAD_DIM)
        shared_keys = lax.dynamic_index_in_dim(prefix_keys, group.astype(jnp.int32), 0, keepdims=False)
        shared_values = lax.dynamic_index_in_dim(prefix_values, group.astype(jnp.int32), 0, keepdims=False)
        shared_keys = shared_keys.astype(jnp.float32).reshape(PREFIX_MAX, KV_HEADS, HEAD_DIM)
        shared_values = shared_values.astype(jnp.float32).reshape(PREFIX_MAX, KV_HEADS, HEAD_DIM)
        shared_length = lax.dynamic_index_in_dim(prefix_length, group.astype(jnp.int32), 0, keepdims=False)
        prefix_scores = jnp.einsum('tkgd,jkd->tkgj', query_rows, shared_keys) * factor
        usable = jnp.arange(PREFIX_MAX, dtype=jnp.int32) < shared_length
        prefix_max, prefix_weights, prefix_total = partial_softmax(prefix_scores, usable)
        rounded = lax.optimization_barrier(prefix_weights.astype(jnp.bfloat16)).astype(jnp.float32)
        prefix_out = (jnp.einsum('tkgj,jkd->tkgd', rounded, shared_values) / prefix_total[..., None]).astype(jnp.bfloat16)
        prefix_lse = prefix_max + jnp.log(prefix_total)
        cached_keys = own_keys.astype(jnp.float32).reshape(SUFFIX_MAX, KV_HEADS, HEAD_DIM)
        cached_values = own_values.astype(jnp.float32).reshape(SUFFIX_MAX, KV_HEADS, HEAD_DIM)
        latest_keys = fresh_keys.astype(jnp.float32).reshape(STEPS, KV_HEADS, HEAD_DIM)
        latest_values = fresh_values.astype(jnp.float32).reshape(STEPS, KV_HEADS, HEAD_DIM)
        suffix_scores = jnp.einsum('tkgd,jkd->tkgj', query_rows, cached_keys) * factor
        latest_scores = jnp.einsum('tkgd,jkd->tkgj', query_rows, latest_keys) * factor
        local_scores = jnp.concatenate([suffix_scores, latest_scores], axis=-1)
        suffix_usable = jnp.broadcast_to(jnp.arange(SUFFIX_MAX, dtype=jnp.int32)[None, :] < own_length, (STEPS, SUFFIX_MAX))
        step_index = jnp.arange(STEPS, dtype=jnp.int32)
        latest_usable = step_index[None, :] <= step_index[:, None]
        local_usable = jnp.concatenate([suffix_usable, latest_usable], axis=-1)[:, None, None, :]
        local_max, local_weights, local_total = partial_softmax(local_scores, local_usable)
        local_rounded = lax.optimization_barrier(local_weights.astype(jnp.bfloat16)).astype(jnp.float32)
        all_values = jnp.concatenate([cached_values, latest_values], axis=0)
        local_out = jnp.einsum('tkgj,jkd->tkgd', local_rounded, all_values)
        highest = jnp.maximum(prefix_lse, local_max)
        prefix_part = jnp.exp(prefix_lse - highest)
        local_part = jnp.exp(local_max - highest)
        prefix_float = lax.optimization_barrier(prefix_out).astype(jnp.float32)
        numerator = prefix_part[..., None] * prefix_float + local_part[..., None] * local_out
        denominator = prefix_part + local_part * local_total
        return (numerator / denominator[..., None]).astype(jnp.bfloat16).reshape(STEPS, HEADS * HEAD_DIM)
    return lax.map(one_request, (queries, new_keys, new_values, suffix_keys, suffix_values, suffix_length, group_of))
```

```python
import functools
import math

import jax
import jax.numpy as jnp
from jax import lax
from jax.experimental import pallas as pl
from jax.experimental.pallas import tpu as pltpu
from jax.sharding import Mesh, PartitionSpec as P

HEADS = 64
KV_HEADS = 8
HEAD_DIM = 128
PREFIX_MAX = 256
STEPS = 2
SUFFIX_MAX = 32
GROUP = HEADS // KV_HEADS
ROWS = GROUP * STEPS
FACTOR = 1.0 / math.sqrt(HEAD_DIM)
Z, Y, CORES, X = 8, 4, 2, 4
LOCAL = 8
HELD = KV_HEADS // X
OWNED = Z * CORES
EARLY = 10
PER_GROUP = 2
REQUESTS = X * LOCAL
BLOCK = PER_GROUP * ROWS
UNITS = OWNED * HELD
OUT_ROWS = UNITS * BLOCK
CACHE_ROWS = 2 * HELD * PREFIX_MAX
CACHE_BLOCK = CACHE_ROWS + 16
F32 = jnp.float32
BF16 = jnp.bfloat16
PARAMS = pltpu.CompilerParams(vmem_limit_bytes=10 * 1024 * 1024)
STAGING = pltpu.CompilerParams(vmem_limit_bytes=32 * 1024 * 1024)


def padded(count):
    return -(-count // 16) * 16


def dot_t(a, b):
    return lax.dot_general(a, b, (((1,), (1,)), ((), ())), preferred_element_type=F32)


def iota(shape, dim):
    return lax.broadcasted_iota(jnp.int32, shape, dim)


def local_kernel(length_ref, q_ref, sk_ref, sv_ref, nk_ref, nv_ref, out_ref, stat_ref):
    width = KV_HEADS * SUFFIX_MAX
    fresh = KV_HEADS * STEPS
    row = iota((HEADS * STEPS, width), 0)
    col = iota((HEADS * STEPS, width), 1)
    same_head = row // ROWS == col // SUFFIX_MAX
    position = col % SUFFIX_MAX
    row2 = iota((HEADS * STEPS, fresh), 0)
    col2 = iota((HEADS * STEPS, fresh), 1)
    seen = jnp.logical_and(row2 // ROWS == col2 // STEPS, col2 % STEPS <= row2 % STEPS)
    lane = iota((HEADS * STEPS, HEAD_DIM), 1)
    columns = jnp.zeros((HEADS * STEPS, HEAD_DIM), F32)
    for r in range(LOCAL):
        q = q_ref[r]
        keys = jnp.concatenate(
            [sk_ref[r, :, k * HEAD_DIM : (k + 1) * HEAD_DIM] for k in range(KV_HEADS)], axis=0
        )
        values = jnp.concatenate(
            [sv_ref[r, :, k * HEAD_DIM : (k + 1) * HEAD_DIM] for k in range(KV_HEADS)], axis=0
        )
        usable = jnp.logical_and(same_head, position < length_ref[r])
        old = jnp.where(usable, dot_t(q, keys) * FACTOR, -jnp.inf)
        new = jnp.where(seen, dot_t(q, nk_ref[r]) * FACTOR, -jnp.inf)
        highest = jnp.maximum(
            jnp.max(old, axis=1, keepdims=True), jnp.max(new, axis=1, keepdims=True)
        )
        old = jnp.exp(old - highest)
        new = jnp.exp(new - highest)
        total = jnp.sum(old, axis=1, keepdims=True) + jnp.sum(new, axis=1, keepdims=True)
        out = jnp.dot(old.astype(BF16), values, preferred_element_type=F32)
        out_ref[r] = out + jnp.dot(new.astype(BF16), nv_ref[r], preferred_element_type=F32)
        columns = jnp.where(lane == r, highest, jnp.where(lane == LOCAL + r, total, columns))
    stat_ref[...] = columns.T[: 2 * LOCAL]


def attend_local(lengths, q, sk, sv, nk, nv):
    vm = pl.BlockSpec(memory_space=pltpu.VMEM)
    shape = jax.ShapeDtypeStruct((LOCAL, HEADS * STEPS, HEAD_DIM), F32)
    return pl.pallas_call(
        local_kernel,
        out_shape=(shape, jax.ShapeDtypeStruct((2 * LOCAL, HEADS * STEPS), F32)),
        in_specs=[pl.BlockSpec(memory_space=pltpu.SMEM)] + [vm] * 5,
        out_specs=(vm, vm),
        compiler_params=PARAMS,
        name="local_attention",
    )(lengths, q, sk, sv, nk, nv)


def split_kernel(x_ref, q_ref, *refs):
    out_refs, sems = refs[:X], refs[X]
    wide = HELD * ROWS
    copies = []
    for s in range(X):
        head = pl.multiple_of(lax.rem(x_ref[0] + s, X) * wide, wide)
        for r in range(LOCAL):
            copies.append(
                pltpu.make_async_copy(
                    q_ref.at[r, pl.ds(head, wide), :],
                    out_refs[s].at[pl.ds(r * wide, wide), :],
                    sems.at[s, r],
                )
            )
    for copy in copies:
        copy.start()
    for copy in copies:
        copy.wait()


def split(x, q):
    part = jax.ShapeDtypeStruct((LOCAL * HELD * ROWS, HEAD_DIM), BF16)
    return pl.pallas_call(
        split_kernel,
        out_shape=[part] * X,
        in_specs=[pl.BlockSpec(memory_space=pltpu.SMEM), pl.BlockSpec(memory_space=pltpu.HBM)],
        out_specs=[pl.BlockSpec(memory_space=pltpu.VMEM)] * X,
        scratch_shapes=[pltpu.SemaphoreType.DMA((X, LOCAL))],
        compiler_params=STAGING,
        name="split_queries",
    )(x, q)


def cache_kernel(length_ref, k_ref, v_ref, cache_ref, sems):
    copies = []
    for i, ref in enumerate((k_ref, v_ref)):
        for h in range(HELD):
            at = (i * HELD + h) * PREFIX_MAX
            copies.append(
                pltpu.make_async_copy(
                    ref.at[0, :, pl.ds(h * HEAD_DIM, HEAD_DIM)],
                    cache_ref.at[pl.ds(at, PREFIX_MAX), :],
                    sems.at[i, h],
                )
            )
    for copy in copies:
        copy.start()
    length = jnp.full((16, HEAD_DIM), length_ref[0], jnp.int32)
    cache_ref[CACHE_ROWS:, :] = length.astype(F32).astype(BF16)
    for copy in copies:
        copy.wait()


def build_cache(length, keys, values):
    hbm = pl.BlockSpec(memory_space=pltpu.HBM)
    return pl.pallas_call(
        cache_kernel,
        out_shape=jax.ShapeDtypeStruct((CACHE_ROWS + 16, HEAD_DIM), BF16),
        in_specs=[pl.BlockSpec(memory_space=pltpu.SMEM)] + [hbm] * 2,
        out_specs=pl.BlockSpec(memory_space=pltpu.VMEM),
        scratch_shapes=[pltpu.SemaphoreType.DMA((2, HELD))],
        compiler_params=STAGING,
        name="build_cache",
    )(length, keys, values)


def stack_kernel(*refs):
    parts, out_ref = refs[:-1], refs[-1]
    size = parts[0].shape[0]
    for i, ref in enumerate(parts):
        out_ref[i * size : (i + 1) * size, :] = ref[...]


def stack(parts):
    vm = pl.BlockSpec(memory_space=pltpu.VMEM)
    size, width = parts[0].shape
    return pl.pallas_call(
        stack_kernel,
        out_shape=jax.ShapeDtypeStruct((len(parts) * size, width), parts[0].dtype),
        in_specs=[vm] * len(parts),
        out_specs=vm,
        compiler_params=PARAMS,
        name="stack_caches",
    )(*parts)


def pack_kernel(place_ref, *refs):
    q_refs, out_refs, packed_ref = refs[:X], refs[X : X + Y], refs[X + Y]
    packed_ref[...] = jnp.zeros(packed_ref.shape, BF16)
    for i in range(REQUESTS):
        for h in range(HELD):
            start = pl.multiple_of((place_ref[i] + h * PER_GROUP) * ROWS, ROWS)
            at = ((i % LOCAL) * HELD + h) * ROWS
            packed_ref[pl.ds(start, ROWS), :] = q_refs[i // LOCAL][at : at + ROWS, :]
    for s in range(Y):
        out_refs[s][...] = packed_ref[s * OUT_ROWS : (s + 1) * OUT_ROWS, :]


def pack(place, queries):
    vm = pl.BlockSpec(memory_space=pltpu.VMEM)
    return pl.pallas_call(
        pack_kernel,
        out_shape=[jax.ShapeDtypeStruct((OUT_ROWS, HEAD_DIM), BF16)] * Y,
        in_specs=[pl.BlockSpec(memory_space=pltpu.SMEM)] + [vm] * X,
        out_specs=[vm] * Y,
        scratch_shapes=[pltpu.VMEM((Y * OUT_ROWS, HEAD_DIM), BF16)],
        compiler_params=PARAMS,
        name="pack_queries",
    )(place, *queries)


def prefix_kernel(first, count, *refs):
    q_refs, caches, out_refs = refs[:Y], refs[Y:-Y], refs[-Y:]
    column = iota((1, PREFIX_MAX), 1).astype(F32)
    lane = iota((Y * BLOCK, HEAD_DIM), 1)
    diagonal = lane % ROWS == iota((Y * BLOCK, HEAD_DIM), 0) % ROWS
    piece = iota((Y * PER_GROUP, HEAD_DIM), 1) // ROWS
    lines = []
    for j in range(count):
        cache, base = caches[j // CORES], j % CORES * CACHE_BLOCK
        length = cache[base + CACHE_ROWS : base + CACHE_BLOCK, :].astype(F32)[:1, :1]
        usable = column < length
        for h in range(HELD):
            unit = (first + j) * HELD + h
            q = jnp.concatenate(
                [ref[unit * BLOCK : (unit + 1) * BLOCK, :] for ref in q_refs], axis=0
            )
            at = base + h * PREFIX_MAX
            keys = cache[at : at + PREFIX_MAX, :]
            at += HELD * PREFIX_MAX
            values = cache[at : at + PREFIX_MAX, :]
            scores = jnp.where(usable, dot_t(q, keys) * FACTOR, -jnp.inf)
            highest = jnp.max(scores, axis=1, keepdims=True)
            weights = jnp.exp(scores - highest)
            total = jnp.sum(weights, axis=1, keepdims=True)
            out = jnp.dot(weights.astype(BF16), values, preferred_element_type=F32)
            out = (out / total).astype(BF16)
            at = (j * HELD + h) * BLOCK
            for s in range(Y):
                out_refs[s][at : at + BLOCK, :] = out[s * BLOCK : (s + 1) * BLOCK]
            log_total = jnp.where(diagonal, highest + jnp.log(total), 0.0)
            line = jnp.sum(log_total.reshape(Y * PER_GROUP, ROWS, HEAD_DIM), axis=1)
            upper = line.astype(BF16).astype(F32)
            remain = line - upper
            middle = remain.astype(BF16).astype(F32)
            lowest = remain - middle
            lines.append(jnp.where(piece == 0, upper, jnp.where(piece == 1, middle, lowest)))
    units = count * HELD
    blank = padded(units * PER_GROUP) - units * PER_GROUP
    for s in range(Y):
        part = [x[s * PER_GROUP : (s + 1) * PER_GROUP] for x in lines]
        if blank:
            part.append(jnp.zeros((blank, HEAD_DIM), F32))
        out_refs[s][units * BLOCK :, :] = jnp.concatenate(part, axis=0).astype(BF16)


def attend_prefix(first, queries, caches):
    count = len(caches) * CORES
    units = count * HELD
    rows = units * BLOCK + padded(units * PER_GROUP)
    vm = pl.BlockSpec(memory_space=pltpu.VMEM)
    return pl.pallas_call(
        functools.partial(prefix_kernel, first, count),
        out_shape=[jax.ShapeDtypeStruct((rows, HEAD_DIM), BF16)] * Y,
        in_specs=[vm] * (Y + len(caches)),
        out_specs=[vm] * Y,
        compiler_params=PARAMS,
        name="prefix_attention_%d" % first,
    )(*queries, *caches)


def unpack_kernel(place_ref, line_ref, *refs):
    early, late = refs[:Y], refs[Y : 2 * Y]
    out_refs, all_ref = refs[2 * Y : 2 * Y + X], refs[2 * Y + X]
    cut = EARLY * HELD * BLOCK
    for s in range(Y):
        base = s * OUT_ROWS
        all_ref[base : base + cut, :] = early[s][:cut, :]
        all_ref[base + cut : base + OUT_ROWS, :] = late[s][: OUT_ROWS - cut, :]
    sources = jnp.concatenate(
        [ref[cut:, :] for ref in early] + [ref[OUT_ROWS - cut :, :] for ref in late], axis=0
    )
    size = LOCAL * HELD
    for i in range(REQUESTS):
        for h in range(HELD):
            rows = pl.ds(pl.multiple_of((place_ref[i] + h * PER_GROUP) * ROWS, ROWS), ROWS)
            at = ((i % LOCAL) * HELD + h) * ROWS
            out_refs[i // LOCAL][at : at + ROWS, :] = all_ref[rows, :]
    wanted = line_ref[...] == iota((REQUESTS * HELD, sources.shape[0]), 1)
    lines = jnp.dot(wanted.astype(BF16), sources, preferred_element_type=F32).astype(BF16)
    for x in range(X):
        out_refs[x][size * ROWS :, :] = lines[x * size : (x + 1) * size]


def unpack(place, line, parts):
    vm = pl.BlockSpec(memory_space=pltpu.VMEM)
    return pl.pallas_call(
        unpack_kernel,
        out_shape=[jax.ShapeDtypeStruct((LOCAL * HELD * (ROWS + 1), HEAD_DIM), BF16)] * X,
        in_specs=[pl.BlockSpec(memory_space=pltpu.SMEM)] + [vm] * (1 + 2 * Y),
        out_specs=[vm] * X,
        scratch_shapes=[pltpu.VMEM((Y * OUT_ROWS, HEAD_DIM), BF16)],
        compiler_params=PARAMS,
        name="unpack_results",
    )(place, line, *parts)


def combine_kernel(x_ref, *refs):
    parts, (local_ref, stat_ref, out_ref, weight_ref) = refs[:X], refs[X:]
    wide = HELD * ROWS
    lane_head = iota((LOCAL, HEAD_DIM), 1) // ROWS
    heads = [lax.rem(x_ref[0] + (X - s), X) * HELD for s in range(X)]
    log_total = jnp.zeros((LOCAL, HEAD_DIM), F32)
    for s in range(X):
        pieces = parts[s][LOCAL * wide :, :].astype(F32)
        lines = pieces + pltpu.roll(pieces, HEAD_DIM - ROWS, 1)
        lines = lines + pltpu.roll(pieces, HEAD_DIM - 2 * ROWS, 1)
        for h in range(HELD):
            head = heads[s] + h
            line = pltpu.roll(lines[h * LOCAL : (h + 1) * LOCAL], head * ROWS, 1)
            log_total = jnp.where(lane_head == head, line, log_total)
    local_max = stat_ref[:LOCAL, :]
    highest = jnp.maximum(log_total, local_max)
    prefix_part = jnp.exp(log_total - highest)
    local_part = jnp.exp(local_max - highest)
    whole = prefix_part + local_part * stat_ref[LOCAL:, :]
    blank = jnp.zeros((HEAD_DIM - 2 * LOCAL, HEAD_DIM), F32)
    weight_ref[...] = jnp.concatenate([prefix_part / whole, local_part / whole, blank], axis=0).T
    for s in range(X):
        rows = pl.ds(pl.multiple_of(heads[s] * ROWS, wide), wide)
        weights = weight_ref[rows, :]
        for r in range(LOCAL):
            prefix = parts[s][r * wide : (r + 1) * wide, :].astype(F32)
            out = weights[:, r : r + 1] * prefix
            out = out + weights[:, LOCAL + r : LOCAL + r + 1] * local_ref[r, rows, :]
            out_ref[r, rows, :] = out.astype(BF16)


def combine(x, parts, local_out, stats):
    vm = pl.BlockSpec(memory_space=pltpu.VMEM)
    return pl.pallas_call(
        combine_kernel,
        out_shape=jax.ShapeDtypeStruct((LOCAL, HEADS * STEPS, HEAD_DIM), BF16),
        in_specs=[pl.BlockSpec(memory_space=pltpu.SMEM)] + [vm] * (X + 2),
        out_specs=vm,
        scratch_shapes=[pltpu.VMEM((HEAD_DIM, HEAD_DIM), F32)],
        compiler_params=PARAMS,
        name="combine_parts",
    )(x, *parts, local_out, stats)


def turn_x(value, turns):
    return lax.ppermute(value, "x", [(i, (i + turns) % X) for i in range(X)])


def shift(value, turns):
    return lax.ppermute(value, "y", [(i, (i + turns) % Y) for i in range(Y)])


def swap_cores(value):
    return lax.ppermute(value, "core", [(i, 1 - i) for i in range(CORES)])


def onward(value):
    pairs = []
    for z in range(Z):
        pairs.append((z * CORES, (z + 1) % Z * CORES))
        pairs.append((z * CORES + 1, (z - 1) % Z * CORES + 1))
    return lax.ppermute(value, ("z", "core"), pairs)


def per_device(
    queries,
    new_keys,
    new_values,
    suffix_keys,
    suffix_values,
    suffix_length,
    group_ids,
    prefix_keys,
    prefix_values,
    prefix_length,
):
    z = lax.axis_index("z")
    core = lax.axis_index("core")
    x = lax.axis_index("x")
    at_x = x.reshape(1).astype(jnp.int32)

    def head_rows(value):
        heads = value.shape[2] // HEAD_DIM
        value = value.reshape(LOCAL, STEPS, heads, HEAD_DIM).transpose(0, 2, 1, 3)
        return value.reshape(LOCAL, heads * STEPS, HEAD_DIM)

    splits = split(at_x, head_rows(queries))
    mine = build_cache(prefix_length, prefix_keys, prefix_values)
    arrived = [splits[0]] + [turn_x(splits[s], s) for s in range(1, X)]

    ids = group_ids[:, 0]
    ids = lax.dynamic_slice_in_dim(jnp.concatenate([ids, ids]), x * LOCAL, REQUESTS)
    index = jnp.arange(REQUESTS, dtype=jnp.int32)
    same = jnp.logical_and(ids[:, None] == ids[None, :], index[:, None] > index[None, :])
    position = jnp.sum(same, axis=1, dtype=jnp.int32)
    turn = ((ids // CORES) % Y - lax.axis_index("y") + Y) % Y
    foreign = (ids % CORES != core).astype(jnp.int32)
    ahead = ids // (CORES * Y) - z
    ahead = (jnp.where(core == 0, -ahead, ahead) + Z) % Z
    near = jnp.where(ahead < Z // 2, 4 * ahead - 2 + foreign, 4 * (Z - ahead) + 1 - foreign)
    arrival = jnp.where(
        ahead == 0, foreign, jnp.where(ahead == Z // 2, OWNED - 2 + foreign, near)
    )
    unit = arrival * (HELD * PER_GROUP) + position
    place = turn * (UNITS * PER_GROUP) + unit
    counts = (EARLY * HELD * PER_GROUP, (OWNED - EARLY) * HELD * PER_GROUP)
    late_line = Y * padded(counts[0]) + turn * padded(counts[1]) + unit - counts[0]
    line = jnp.where(arrival < EARLY, turn * padded(counts[0]) + unit, late_line)
    line = line.reshape(X, 1, LOCAL) + jnp.arange(HELD, dtype=jnp.int32)[:, None] * PER_GROUP
    line = line.reshape(REQUESTS * HELD, 1)

    packed = pack(place, [arrived[-s % X] for s in range(X)])
    received = [packed[0]] + [shift(packed[s], s) for s in range(1, Y)]

    pair_0 = stack([mine, swap_cores(mine)])
    pair_1 = onward(pair_0)
    pair_2 = onward(pair_1)
    pair_2, received[1], received[3] = lax.optimization_barrier((pair_2, received[1], received[3]))
    pair_3 = onward(pair_2)
    local_queries, received[1] = lax.optimization_barrier((head_rows(queries), received[1]))
    local_out, stats = attend_local(
        suffix_length,
        local_queries,
        suffix_keys,
        suffix_values,
        head_rows(new_keys),
        head_rows(new_values),
    )
    pair_3, local_out, stats, *received = lax.optimization_barrier(
        (pair_3, local_out, stats, *received)
    )
    pair_4 = onward(pair_3)
    early = attend_prefix(0, received, [pair_0, pair_1, swap_cores(pair_1), pair_2, swap_cores(pair_2)])
    late = attend_prefix(EARLY, received, [pair_3, swap_cores(pair_3), pair_4])
    parts = []
    for results in (early, late):
        parts += [results[0]] + [shift(results[s], -s) for s in range(1, Y)]

    pieces = unpack(place, line, parts)
    got = [pieces[0]] + [turn_x(pieces[s], s) for s in range(1, X)]
    out = combine(at_x, got, local_out, stats)
    out = out.reshape(LOCAL, HEADS, STEPS, HEAD_DIM).transpose(0, 2, 1, 3)
    return out.reshape(LOCAL, STEPS, HEADS * HEAD_DIM)


def solution(mesh):
    axes = ("z", "y", "core", "x")
    fine = Mesh(mesh.devices.reshape(Z, Y, CORES, X), axes)
    rows = P(axes, None, None)
    groups = ("z", "y", "core")
    placed = (rows,) * 5 + (
        P(axes),
        P(groups, None),
        P(groups, None, "x"),
        P(groups, None, "x"),
        P(groups),
    )
    return jax.shard_map(
        per_device, mesh=fine, in_specs=placed, out_specs=rows, check_vma=False
    )
```

```python
import functools
import math

import jax
import jax.numpy as jnp
from jax import lax
from jax.experimental import pallas as pl
from jax.experimental.pallas import tpu as pltpu
from jax.sharding import Mesh, PartitionSpec as P

HEADS = 64
KV_HEADS = 8
HEAD_DIM = 128
PREFIX_MAX = 256
STEPS = 2
SUFFIX_MAX = 32
GROUP = HEADS // KV_HEADS
ROWS = GROUP * STEPS
FACTOR = 1.0 / math.sqrt(HEAD_DIM)
Z, Y, CORES, X = 8, 4, 2, 4
LOCAL = 8
HELD = KV_HEADS // X
OWNED = Z * CORES
EARLY = 10
PER_GROUP = 2
REQUESTS = X * LOCAL
BLOCK = PER_GROUP * ROWS
UNITS = OWNED * HELD
OUT_ROWS = UNITS * BLOCK
CACHE_ROWS = 2 * HELD * PREFIX_MAX
CACHE_BLOCK = CACHE_ROWS + 16
F32 = jnp.float32
BF16 = jnp.bfloat16
PARAMS = pltpu.CompilerParams(vmem_limit_bytes=10 * 1024 * 1024)
STAGING = pltpu.CompilerParams(vmem_limit_bytes=32 * 1024 * 1024)


def padded(count):
    return -(-count // 16) * 16


def dot_t(a, b):
    return lax.dot_general(a, b, (((1,), (1,)), ((), ())), preferred_element_type=F32)


def iota(shape, dim):
    return lax.broadcasted_iota(jnp.int32, shape, dim)


def local_kernel(length_ref, q_ref, sk_ref, sv_ref, nk_ref, nv_ref, out_ref, stat_ref):
    width = KV_HEADS * SUFFIX_MAX
    fresh = KV_HEADS * STEPS
    row = iota((HEADS * STEPS, width), 0)
    col = iota((HEADS * STEPS, width), 1)
    same_head = row // ROWS == col // SUFFIX_MAX
    position = col % SUFFIX_MAX
    row2 = iota((HEADS * STEPS, fresh), 0)
    col2 = iota((HEADS * STEPS, fresh), 1)
    seen = jnp.logical_and(row2 // ROWS == col2 // STEPS, col2 % STEPS <= row2 % STEPS)
    lane = iota((HEADS * STEPS, HEAD_DIM), 1)
    columns = jnp.zeros((HEADS * STEPS, HEAD_DIM), F32)
    for r in range(LOCAL):
        q = q_ref[r]
        keys = jnp.concatenate(
            [sk_ref[r, :, k * HEAD_DIM : (k + 1) * HEAD_DIM] for k in range(KV_HEADS)], axis=0
        )
        values = jnp.concatenate(
            [sv_ref[r, :, k * HEAD_DIM : (k + 1) * HEAD_DIM] for k in range(KV_HEADS)], axis=0
        )
        usable = jnp.logical_and(same_head, position < length_ref[r])
        old = jnp.where(usable, dot_t(q, keys) * FACTOR, -jnp.inf)
        new = jnp.where(seen, dot_t(q, nk_ref[r]) * FACTOR, -jnp.inf)
        highest = jnp.maximum(
            jnp.max(old, axis=1, keepdims=True), jnp.max(new, axis=1, keepdims=True)
        )
        old = jnp.exp(old - highest)
        new = jnp.exp(new - highest)
        total = jnp.sum(old, axis=1, keepdims=True) + jnp.sum(new, axis=1, keepdims=True)
        out = jnp.dot(old.astype(BF16), values, preferred_element_type=F32)
        out_ref[r] = out + jnp.dot(new.astype(BF16), nv_ref[r], preferred_element_type=F32)
        columns = jnp.where(lane == r, highest, jnp.where(lane == LOCAL + r, total, columns))
    stat_ref[...] = columns.T[: 2 * LOCAL]


def attend_local(lengths, q, sk, sv, nk, nv):
    vm = pl.BlockSpec(memory_space=pltpu.VMEM)
    shape = jax.ShapeDtypeStruct((LOCAL, HEADS * STEPS, HEAD_DIM), F32)
    return pl.pallas_call(
        local_kernel,
        out_shape=(shape, jax.ShapeDtypeStruct((2 * LOCAL, HEADS * STEPS), F32)),
        in_specs=[pl.BlockSpec(memory_space=pltpu.SMEM)] + [vm] * 5,
        out_specs=(vm, vm),
        compiler_params=PARAMS,
        name="local_attention",
    )(lengths, q, sk, sv, nk, nv)


def split_kernel(x_ref, q_ref, *refs):
    out_refs, sems = refs[:X], refs[X]
    wide = HELD * ROWS
    copies = []
    for s in range(X):
        head = pl.multiple_of(lax.rem(x_ref[0] + s, X) * wide, wide)
        for r in range(LOCAL):
            copies.append(
                pltpu.make_async_copy(
                    q_ref.at[r, pl.ds(head, wide), :],
                    out_refs[s].at[pl.ds(r * wide, wide), :],
                    sems.at[s, r],
                )
            )
    for copy in copies:
        copy.start()
    for copy in copies:
        copy.wait()


def split(x, q):
    part = jax.ShapeDtypeStruct((LOCAL * HELD * ROWS, HEAD_DIM), BF16)
    return pl.pallas_call(
        split_kernel,
        out_shape=[part] * X,
        in_specs=[pl.BlockSpec(memory_space=pltpu.SMEM), pl.BlockSpec(memory_space=pltpu.HBM)],
        out_specs=[pl.BlockSpec(memory_space=pltpu.VMEM)] * X,
        scratch_shapes=[pltpu.SemaphoreType.DMA((X, LOCAL))],
        compiler_params=STAGING,
        name="split_queries",
    )(x, q)


def cache_kernel(length_ref, k_ref, v_ref, cache_ref, sems):
    copies = []
    for i, ref in enumerate((k_ref, v_ref)):
        for h in range(HELD):
            at = (i * HELD + h) * PREFIX_MAX
            copies.append(
                pltpu.make_async_copy(
                    ref.at[0, :, pl.ds(h * HEAD_DIM, HEAD_DIM)],
                    cache_ref.at[pl.ds(at, PREFIX_MAX), :],
                    sems.at[i, h],
                )
            )
    for copy in copies:
        copy.start()
    length = jnp.full((16, HEAD_DIM), length_ref[0], jnp.int32)
    cache_ref[CACHE_ROWS:, :] = length.astype(F32).astype(BF16)
    for copy in copies:
        copy.wait()


def build_cache(length, keys, values):
    hbm = pl.BlockSpec(memory_space=pltpu.HBM)
    return pl.pallas_call(
        cache_kernel,
        out_shape=jax.ShapeDtypeStruct((CACHE_ROWS + 16, HEAD_DIM), BF16),
        in_specs=[pl.BlockSpec(memory_space=pltpu.SMEM)] + [hbm] * 2,
        out_specs=pl.BlockSpec(memory_space=pltpu.VMEM),
        scratch_shapes=[pltpu.SemaphoreType.DMA((2, HELD))],
        compiler_params=STAGING,
        name="build_cache",
    )(length, keys, values)


def stack_kernel(*refs):
    parts, out_ref = refs[:-1], refs[-1]
    size = parts[0].shape[0]
    for i, ref in enumerate(parts):
        out_ref[i * size : (i + 1) * size, :] = ref[...]


def stack(parts):
    vm = pl.BlockSpec(memory_space=pltpu.VMEM)
    size, width = parts[0].shape
    return pl.pallas_call(
        stack_kernel,
        out_shape=jax.ShapeDtypeStruct((len(parts) * size, width), parts[0].dtype),
        in_specs=[vm] * len(parts),
        out_specs=vm,
        compiler_params=PARAMS,
        name="stack_caches",
    )(*parts)


def pack_kernel(place_ref, *refs):
    q_refs, out_refs, packed_ref = refs[:X], refs[X : X + Y], refs[X + Y]
    packed_ref[...] = jnp.zeros(packed_ref.shape, BF16)
    for i in range(REQUESTS):
        for h in range(HELD):
            start = pl.multiple_of((place_ref[i] + h * PER_GROUP) * ROWS, ROWS)
            at = ((i % LOCAL) * HELD + h) * ROWS
            packed_ref[pl.ds(start, ROWS), :] = q_refs[i // LOCAL][at : at + ROWS, :]
    for s in range(Y):
        out_refs[s][...] = packed_ref[s * OUT_ROWS : (s + 1) * OUT_ROWS, :]


def pack(place, queries):
    vm = pl.BlockSpec(memory_space=pltpu.VMEM)
    return pl.pallas_call(
        pack_kernel,
        out_shape=[jax.ShapeDtypeStruct((OUT_ROWS, HEAD_DIM), BF16)] * Y,
        in_specs=[pl.BlockSpec(memory_space=pltpu.SMEM)] + [vm] * X,
        out_specs=[vm] * Y,
        scratch_shapes=[pltpu.VMEM((Y * OUT_ROWS, HEAD_DIM), BF16)],
        compiler_params=PARAMS,
        name="pack_queries",
    )(place, *queries)


def prefix_kernel(first, count, *refs):
    q_refs, caches, out_refs = refs[:Y], refs[Y:-Y], refs[-Y:]
    column = iota((1, PREFIX_MAX), 1).astype(F32)
    lane = iota((Y * BLOCK, HEAD_DIM), 1)
    diagonal = lane % ROWS == iota((Y * BLOCK, HEAD_DIM), 0) % ROWS
    piece = iota((Y * PER_GROUP, HEAD_DIM), 1) // ROWS
    lines = []
    for j in range(count):
        cache, base = caches[j // CORES], j % CORES * CACHE_BLOCK
        length = cache[base + CACHE_ROWS : base + CACHE_BLOCK, :].astype(F32)[:1, :1]
        usable = column < length
        for h in range(HELD):
            unit = (first + j) * HELD + h
            q = jnp.concatenate(
                [ref[unit * BLOCK : (unit + 1) * BLOCK, :] for ref in q_refs], axis=0
            )
            at = base + h * PREFIX_MAX
            keys = cache[at : at + PREFIX_MAX, :]
            at += HELD * PREFIX_MAX
            values = cache[at : at + PREFIX_MAX, :]
            scores = jnp.where(usable, dot_t(q, keys) * FACTOR, -jnp.inf)
            highest = jnp.max(scores, axis=1, keepdims=True)
            weights = jnp.exp(scores - highest)
            total = jnp.sum(weights, axis=1, keepdims=True)
            out = jnp.dot(weights.astype(BF16), values, preferred_element_type=F32)
            out = (out / total).astype(BF16)
            at = (j * HELD + h) * BLOCK
            for s in range(Y):
                out_refs[s][at : at + BLOCK, :] = out[s * BLOCK : (s + 1) * BLOCK]
            log_total = jnp.where(diagonal, highest + jnp.log(total), 0.0)
            line = jnp.sum(log_total.reshape(Y * PER_GROUP, ROWS, HEAD_DIM), axis=1)
            upper = line.astype(BF16).astype(F32)
            remain = line - upper
            middle = remain.astype(BF16).astype(F32)
            lowest = remain - middle
            lines.append(jnp.where(piece == 0, upper, jnp.where(piece == 1, middle, lowest)))
    units = count * HELD
    blank = padded(units * PER_GROUP) - units * PER_GROUP
    for s in range(Y):
        part = [x[s * PER_GROUP : (s + 1) * PER_GROUP] for x in lines]
        if blank:
            part.append(jnp.zeros((blank, HEAD_DIM), F32))
        out_refs[s][units * BLOCK :, :] = jnp.concatenate(part, axis=0).astype(BF16)


def attend_prefix(first, queries, caches):
    count = len(caches) * CORES
    units = count * HELD
    rows = units * BLOCK + padded(units * PER_GROUP)
    vm = pl.BlockSpec(memory_space=pltpu.VMEM)
    return pl.pallas_call(
        functools.partial(prefix_kernel, first, count),
        out_shape=[jax.ShapeDtypeStruct((rows, HEAD_DIM), BF16)] * Y,
        in_specs=[vm] * (Y + len(caches)),
        out_specs=[vm] * Y,
        compiler_params=PARAMS,
        name="prefix_attention_%d" % first,
    )(*queries, *caches)


def unpack_kernel(place_ref, line_ref, *refs):
    early, late = refs[:Y], refs[Y : 2 * Y]
    out_refs, all_ref = refs[2 * Y : 2 * Y + X], refs[2 * Y + X]
    cut = EARLY * HELD * BLOCK
    for s in range(Y):
        base = s * OUT_ROWS
        all_ref[base : base + cut, :] = early[s][:cut, :]
        all_ref[base + cut : base + OUT_ROWS, :] = late[s][: OUT_ROWS - cut, :]
    sources = jnp.concatenate(
        [ref[cut:, :] for ref in early] + [ref[OUT_ROWS - cut :, :] for ref in late], axis=0
    )
    size = LOCAL * HELD
    for i in range(REQUESTS):
        for h in range(HELD):
            rows = pl.ds(pl.multiple_of((place_ref[i] + h * PER_GROUP) * ROWS, ROWS), ROWS)
            at = ((i % LOCAL) * HELD + h) * ROWS
            out_refs[i // LOCAL][at : at + ROWS, :] = all_ref[rows, :]
    wanted = line_ref[...] == iota((REQUESTS * HELD, sources.shape[0]), 1)
    lines = jnp.dot(wanted.astype(BF16), sources, preferred_element_type=F32).astype(BF16)
    for x in range(X):
        out_refs[x][size * ROWS :, :] = lines[x * size : (x + 1) * size]


def unpack(place, line, parts):
    vm = pl.BlockSpec(memory_space=pltpu.VMEM)
    return pl.pallas_call(
        unpack_kernel,
        out_shape=[jax.ShapeDtypeStruct((LOCAL * HELD * (ROWS + 1), HEAD_DIM), BF16)] * X,
        in_specs=[pl.BlockSpec(memory_space=pltpu.SMEM)] + [vm] * (1 + 2 * Y),
        out_specs=[vm] * X,
        scratch_shapes=[pltpu.VMEM((Y * OUT_ROWS, HEAD_DIM), BF16)],
        compiler_params=PARAMS,
        name="unpack_results",
    )(place, line, *parts)


def combine_kernel(x_ref, *refs):
    parts, (local_ref, stat_ref, out_ref, weight_ref) = refs[:X], refs[X:]
    wide = HELD * ROWS
    lane_head = iota((LOCAL, HEAD_DIM), 1) // ROWS
    heads = [lax.rem(x_ref[0] + (X - s), X) * HELD for s in range(X)]
    log_total = jnp.zeros((LOCAL, HEAD_DIM), F32)
    for s in range(X):
        pieces = parts[s][LOCAL * wide :, :].astype(F32)
        lines = pieces + pltpu.roll(pieces, HEAD_DIM - ROWS, 1)
        lines = lines + pltpu.roll(pieces, HEAD_DIM - 2 * ROWS, 1)
        for h in range(HELD):
            head = heads[s] + h
            line = pltpu.roll(lines[h * LOCAL : (h + 1) * LOCAL], head * ROWS, 1)
            log_total = jnp.where(lane_head == head, line, log_total)
    local_max = stat_ref[:LOCAL, :]
    highest = jnp.maximum(log_total, local_max)
    prefix_part = jnp.exp(log_total - highest)
    local_part = jnp.exp(local_max - highest)
    whole = prefix_part + local_part * stat_ref[LOCAL:, :]
    blank = jnp.zeros((HEAD_DIM - 2 * LOCAL, HEAD_DIM), F32)
    weight_ref[...] = jnp.concatenate([prefix_part / whole, local_part / whole, blank], axis=0).T
    for s in range(X):
        rows = pl.ds(pl.multiple_of(heads[s] * ROWS, wide), wide)
        weights = weight_ref[rows, :]
        for r in range(LOCAL):
            prefix = parts[s][r * wide : (r + 1) * wide, :].astype(F32)
            out = weights[:, r : r + 1] * prefix
            out = out + weights[:, LOCAL + r : LOCAL + r + 1] * local_ref[r, rows, :]
            out_ref[r, rows, :] = out.astype(BF16)


def combine(x, parts, local_out, stats):
    vm = pl.BlockSpec(memory_space=pltpu.VMEM)
    return pl.pallas_call(
        combine_kernel,
        out_shape=jax.ShapeDtypeStruct((LOCAL, HEADS * STEPS, HEAD_DIM), BF16),
        in_specs=[pl.BlockSpec(memory_space=pltpu.SMEM)] + [vm] * (X + 2),
        out_specs=vm,
        scratch_shapes=[pltpu.VMEM((HEAD_DIM, HEAD_DIM), F32)],
        compiler_params=PARAMS,
        name="combine_parts",
    )(x, *parts, local_out, stats)


def turn_x(value, turns):
    return lax.ppermute(value, "x", [(i, (i + turns) % X) for i in range(X)])


def shift(value, turns):
    return lax.ppermute(value, "y", [(i, (i + turns) % Y) for i in range(Y)])


def swap_cores(value):
    return lax.ppermute(value, "core", [(i, 1 - i) for i in range(CORES)])


def onward(value):
    pairs = []
    for z in range(Z):
        pairs.append((z * CORES, (z + 1) % Z * CORES))
        pairs.append((z * CORES + 1, (z - 1) % Z * CORES + 1))
    return lax.ppermute(value, ("z", "core"), pairs)


def per_device(
    queries,
    new_keys,
    new_values,
    suffix_keys,
    suffix_values,
    suffix_length,
    group_ids,
    prefix_keys,
    prefix_values,
    prefix_length,
):
    z = lax.axis_index("z")
    core = lax.axis_index("core")
    x = lax.axis_index("x")
    at_x = x.reshape(1).astype(jnp.int32)

    def head_rows(value):
        heads = value.shape[2] // HEAD_DIM
        value = value.reshape(LOCAL, STEPS, heads, HEAD_DIM).transpose(0, 2, 1, 3)
        return value.reshape(LOCAL, heads * STEPS, HEAD_DIM)

    splits = list(split(at_x, head_rows(queries)))
    mine = build_cache(prefix_length, prefix_keys, prefix_values)
    arrived = [splits[0]] + [turn_x(splits[s], s) for s in range(1, X)]

    ids = group_ids[:, 0]
    ids = lax.dynamic_slice_in_dim(jnp.concatenate([ids, ids]), x * LOCAL, REQUESTS)
    index = jnp.arange(REQUESTS, dtype=jnp.int32)
    same = jnp.logical_and(ids[:, None] == ids[None, :], index[:, None] > index[None, :])
    position = jnp.sum(same, axis=1, dtype=jnp.int32)
    turn = ((ids // CORES) % Y - lax.axis_index("y") + Y) % Y
    foreign = (ids % CORES != core).astype(jnp.int32)
    ahead = ids // (CORES * Y) - z
    ahead = (jnp.where(core == 0, -ahead, ahead) + Z) % Z
    near = jnp.where(ahead < Z // 2, 4 * ahead - 2 + foreign, 4 * (Z - ahead) + 1 - foreign)
    arrival = jnp.where(
        ahead == 0, foreign, jnp.where(ahead == Z // 2, OWNED - 2 + foreign, near)
    )
    unit = arrival * (HELD * PER_GROUP) + position
    place = turn * (UNITS * PER_GROUP) + unit
    counts = (EARLY * HELD * PER_GROUP, (OWNED - EARLY) * HELD * PER_GROUP)
    late_line = Y * padded(counts[0]) + turn * padded(counts[1]) + unit - counts[0]
    line = jnp.where(arrival < EARLY, turn * padded(counts[0]) + unit, late_line)
    line = line.reshape(X, 1, LOCAL) + jnp.arange(HELD, dtype=jnp.int32)[:, None] * PER_GROUP
    line = line.reshape(REQUESTS * HELD, 1)

    packed = pack(place, [arrived[-s % X] for s in range(X)])
    received = [packed[0]] + [shift(packed[s], s) for s in range(1, Y)]

    pair_0 = stack([mine, swap_cores(mine)])
    pair_1 = onward(pair_0)
    local_queries, splits[0] = lax.optimization_barrier((head_rows(queries), splits[0]))
    local_out, stats = attend_local(
        suffix_length,
        local_queries,
        suffix_keys,
        suffix_values,
        head_rows(new_keys),
        head_rows(new_values),
    )
    pair_1, local_out, stats = lax.optimization_barrier((pair_1, local_out, stats))
    pair_2 = onward(pair_1)
    pair_2, received[1], received[3] = lax.optimization_barrier((pair_2, received[1], received[3]))
    pair_3 = onward(pair_2)
    pair_3, *received = lax.optimization_barrier((pair_3, *received))
    pair_4 = onward(pair_3)
    early = attend_prefix(0, received, [pair_0, pair_1, swap_cores(pair_1), pair_2, swap_cores(pair_2)])
    late = attend_prefix(EARLY, received, [pair_3, swap_cores(pair_3), pair_4])
    parts = []
    for results in (early, late):
        parts += [results[0]] + [shift(results[s], -s) for s in range(1, Y)]

    pieces = unpack(place, line, parts)
    got = [pieces[0]] + [turn_x(pieces[s], s) for s in range(1, X)]
    out = combine(at_x, got, local_out, stats)
    out = out.reshape(LOCAL, HEADS, STEPS, HEAD_DIM).transpose(0, 2, 1, 3)
    return out.reshape(LOCAL, STEPS, HEADS * HEAD_DIM)


def solution(mesh):
    axes = ("z", "y", "core", "x")
    fine = Mesh(mesh.devices.reshape(Z, Y, CORES, X), axes)
    rows = P(axes, None, None)
    groups = ("z", "y", "core")
    placed = (rows,) * 5 + (
        P(axes),
        P(groups, None),
        P(groups, None, "x"),
        P(groups, None, "x"),
        P(groups),
    )
    return jax.shard_map(
        per_device, mesh=fine, in_specs=placed, out_specs=rows, check_vma=False
    )
```

```python
import functools
import math

import jax
import jax.numpy as jnp
from jax import lax
from jax.experimental import pallas as pl
from jax.experimental.pallas import tpu as pltpu
from jax.sharding import Mesh, PartitionSpec as P

HEADS = 64
KV_HEADS = 8
HEAD_DIM = 128
PREFIX_MAX = 256
STEPS = 2
SUFFIX_MAX = 32
GROUP = HEADS // KV_HEADS
ROWS = GROUP * STEPS
FACTOR = 1.0 / math.sqrt(HEAD_DIM)
Z, Y, CORES, X = 8, 4, 2, 4
PEERS = CORES * X
LOCAL = 8
COLUMN = PEERS * LOCAL
HELD = KV_HEADS // X
OWNED = Z
EARLY = 5
PER_GROUP = 4
BLOCK = PER_GROUP * ROWS
UNITS = OWNED * HELD
OUT_ROWS = UNITS * BLOCK
DUMP = Y * OUT_ROWS // ROWS
CACHE_ROWS = 2 * HELD * PREFIX_MAX
F32 = jnp.float32
BF16 = jnp.bfloat16
PARAMS = pltpu.CompilerParams(vmem_limit_bytes=32 * 1024 * 1024)


def padded(count):
    return -(-count // 16) * 16


def dot_t(a, b):
    return lax.dot_general(a, b, (((1,), (1,)), ((), ())), preferred_element_type=F32)


def iota(shape, dim):
    return lax.broadcasted_iota(jnp.int32, shape, dim)


def local_kernel(length_ref, q_ref, sk_ref, sv_ref, nk_ref, nv_ref, out_ref, stat_ref):
    width = KV_HEADS * SUFFIX_MAX
    fresh = KV_HEADS * STEPS
    row = iota((HEADS * STEPS, width), 0)
    col = iota((HEADS * STEPS, width), 1)
    same_head = row // ROWS == col // SUFFIX_MAX
    position = col % SUFFIX_MAX
    row2 = iota((HEADS * STEPS, fresh), 0)
    col2 = iota((HEADS * STEPS, fresh), 1)
    seen = jnp.logical_and(row2 // ROWS == col2 // STEPS, col2 % STEPS <= row2 % STEPS)
    lane = iota((HEADS * STEPS, HEAD_DIM), 1)
    columns = jnp.zeros((HEADS * STEPS, HEAD_DIM), F32)
    for r in range(LOCAL):
        q = q_ref[r]
        keys = jnp.concatenate(
            [sk_ref[r, :, k * HEAD_DIM : (k + 1) * HEAD_DIM] for k in range(KV_HEADS)], axis=0
        )
        values = jnp.concatenate(
            [sv_ref[r, :, k * HEAD_DIM : (k + 1) * HEAD_DIM] for k in range(KV_HEADS)], axis=0
        )
        usable = jnp.logical_and(same_head, position < length_ref[r])
        old = jnp.where(usable, dot_t(q, keys) * FACTOR, -jnp.inf)
        new = jnp.where(seen, dot_t(q, nk_ref[r]) * FACTOR, -jnp.inf)
        highest = jnp.maximum(
            jnp.max(old, axis=1, keepdims=True), jnp.max(new, axis=1, keepdims=True)
        )
        old = jnp.exp(old - highest)
        new = jnp.exp(new - highest)
        total = jnp.sum(old, axis=1, keepdims=True) + jnp.sum(new, axis=1, keepdims=True)
        out = jnp.dot(old.astype(BF16), values, preferred_element_type=F32)
        out_ref[r] = out + jnp.dot(new.astype(BF16), nv_ref[r], preferred_element_type=F32)
        columns = jnp.where(lane == r, highest, jnp.where(lane == LOCAL + r, total, columns))
    stat_ref[...] = columns.T[: 2 * LOCAL]


def attend_local(lengths, q, sk, sv, nk, nv):
    vm = pl.BlockSpec(memory_space=pltpu.VMEM)
    shape = jax.ShapeDtypeStruct((LOCAL, HEADS * STEPS, HEAD_DIM), F32)
    return pl.pallas_call(
        local_kernel,
        out_shape=(shape, jax.ShapeDtypeStruct((2 * LOCAL, HEADS * STEPS), F32)),
        in_specs=[pl.BlockSpec(memory_space=pltpu.SMEM)] + [vm] * 5,
        out_specs=(vm, vm),
        compiler_params=PARAMS,
        name="local_attention",
    )(lengths, q, sk, sv, nk, nv)


def split_kernel(x_ref, q_ref, *refs):
    out_refs, sems = refs[:X], refs[X]
    wide = HELD * ROWS
    copies = []
    for s in range(X):
        head = pl.multiple_of(lax.rem(x_ref[0] + s, X) * wide, wide)
        for r in range(LOCAL):
            copies.append(
                pltpu.make_async_copy(
                    q_ref.at[r, pl.ds(head, wide), :],
                    out_refs[s].at[pl.ds(r * wide, wide), :],
                    sems.at[s, r],
                )
            )
    for copy in copies:
        copy.start()
    for copy in copies:
        copy.wait()


def split(x, q):
    part = jax.ShapeDtypeStruct((LOCAL * HELD * ROWS, HEAD_DIM), BF16)
    return pl.pallas_call(
        split_kernel,
        out_shape=[part] * X,
        in_specs=[pl.BlockSpec(memory_space=pltpu.SMEM), pl.BlockSpec(memory_space=pl.ANY)],
        out_specs=[pl.BlockSpec(memory_space=pltpu.VMEM)] * X,
        scratch_shapes=[pltpu.SemaphoreType.DMA((X, LOCAL))],
        compiler_params=PARAMS,
        name="split_queries",
    )(x, q)


def cache_kernel(length_ref, k_ref, v_ref, after_ref, cache_ref, sems):
    copies = []
    for i, ref in enumerate((k_ref, v_ref)):
        for h in range(HELD):
            at = (i * HELD + h) * PREFIX_MAX
            copies.append(
                pltpu.make_async_copy(
                    ref.at[0, :, pl.ds(h * HEAD_DIM, HEAD_DIM)],
                    cache_ref.at[pl.ds(at, PREFIX_MAX), :],
                    sems.at[i, h],
                )
            )
    for copy in copies:
        copy.start()
    length = jnp.full((16, HEAD_DIM), length_ref[0], jnp.int32)
    cache_ref[CACHE_ROWS:, :] = length.astype(F32).astype(BF16)
    for copy in copies:
        copy.wait()


def build_cache(length, keys, values, after):
    anywhere = pl.BlockSpec(memory_space=pl.ANY)
    return pl.pallas_call(
        cache_kernel,
        out_shape=jax.ShapeDtypeStruct((CACHE_ROWS + 16, HEAD_DIM), BF16),
        in_specs=[pl.BlockSpec(memory_space=pltpu.SMEM)] + [anywhere] * 3,
        out_specs=pl.BlockSpec(memory_space=pltpu.VMEM),
        scratch_shapes=[pltpu.SemaphoreType.DMA((2, HELD))],
        compiler_params=PARAMS,
        name="build_cache",
    )(length, keys, values, after)


def stack_kernel(*refs):
    parts, out_ref = refs[:-1], refs[-1]
    size = parts[0].shape[0]
    for i, ref in enumerate(parts):
        out_ref[i * size : (i + 1) * size, :] = ref[...]


def stack(parts):
    vm = pl.BlockSpec(memory_space=pltpu.VMEM)
    size, width = parts[0].shape
    return pl.pallas_call(
        stack_kernel,
        out_shape=jax.ShapeDtypeStruct((len(parts) * size, width), parts[0].dtype),
        in_specs=[vm] * len(parts),
        out_specs=vm,
        compiler_params=PARAMS,
        name="stack_queries",
    )(*parts)


def pack_kernel(place_ref, own_ref, other_ref, *out_refs):
    packed_ref = out_refs[Y]
    packed_ref[...] = jnp.zeros(packed_ref.shape, BF16)
    half = COLUMN // CORES
    for i in range(COLUMN):
        q_ref = own_ref if i < half else other_ref
        for h in range(HELD):
            start = pl.multiple_of((place_ref[i] + h * PER_GROUP) * ROWS, ROWS)
            at = ((i % half) * HELD + h) * ROWS
            packed_ref[pl.ds(start, ROWS), :] = q_ref[at : at + ROWS, :]
    for s in range(Y):
        out_refs[s][...] = packed_ref[s * OUT_ROWS : (s + 1) * OUT_ROWS, :]


def pack(place, own, other):
    vm = pl.BlockSpec(memory_space=pltpu.VMEM)
    return pl.pallas_call(
        pack_kernel,
        out_shape=[jax.ShapeDtypeStruct((OUT_ROWS, HEAD_DIM), BF16)] * Y,
        in_specs=[pl.BlockSpec(memory_space=pltpu.SMEM), vm, vm],
        out_specs=[vm] * Y,
        scratch_shapes=[pltpu.VMEM((Y * OUT_ROWS + 2 * BLOCK, HEAD_DIM), BF16)],
        compiler_params=PARAMS,
        name="pack_queries",
    )(place, own, other)


def prefix_kernel(first, count, *refs):
    q_refs, caches, out_refs = refs[:Y], refs[Y : Y + count], refs[Y + count :]
    column = iota((1, PREFIX_MAX), 1).astype(F32)
    lane = iota((Y * BLOCK, HEAD_DIM), 1)
    diagonal = lane % ROWS == iota((Y * BLOCK, HEAD_DIM), 0) % ROWS
    piece = iota((Y * PER_GROUP, HEAD_DIM), 1) // ROWS
    lines = []
    for j in range(count):
        length = caches[j][CACHE_ROWS:, :].astype(F32)[:1, :1]
        usable = column < length
        for h in range(HELD):
            unit = (first + j) * HELD + h
            q = jnp.concatenate(
                [ref[unit * BLOCK : (unit + 1) * BLOCK, :] for ref in q_refs], axis=0
            )
            keys = caches[j][h * PREFIX_MAX : (h + 1) * PREFIX_MAX, :]
            values = caches[j][(HELD + h) * PREFIX_MAX : (HELD + h + 1) * PREFIX_MAX, :]
            scores = jnp.where(usable, dot_t(q, keys) * FACTOR, -jnp.inf)
            highest = jnp.max(scores, axis=1, keepdims=True)
            weights = jnp.exp(scores - highest)
            total = jnp.sum(weights, axis=1, keepdims=True)
            out = jnp.dot(weights.astype(BF16), values, preferred_element_type=F32)
            out = (out / total).astype(BF16)
            at = (j * HELD + h) * BLOCK
            for s in range(Y):
                out_refs[s][at : at + BLOCK, :] = out[s * BLOCK : (s + 1) * BLOCK]
            log_total = jnp.where(diagonal, highest + jnp.log(total), 0.0)
            line = jnp.sum(log_total.reshape(Y * PER_GROUP, ROWS, HEAD_DIM), axis=1)
            upper = line.astype(BF16).astype(F32)
            remain = line - upper
            middle = remain.astype(BF16).astype(F32)
            lowest = remain - middle
            lines.append(jnp.where(piece == 0, upper, jnp.where(piece == 1, middle, lowest)))
    units = count * HELD
    blank = padded(units * PER_GROUP) - units * PER_GROUP
    for s in range(Y):
        part = [x[s * PER_GROUP : (s + 1) * PER_GROUP] for x in lines]
        if blank:
            part.append(jnp.zeros((blank, HEAD_DIM), F32))
        out_refs[s][units * BLOCK :, :] = jnp.concatenate(part, axis=0).astype(BF16)


def attend_prefix(first, queries, caches):
    count = len(caches)
    units = count * HELD
    rows = units * BLOCK + padded(units * PER_GROUP)
    vm = pl.BlockSpec(memory_space=pltpu.VMEM)
    return pl.pallas_call(
        functools.partial(prefix_kernel, first, count),
        out_shape=[jax.ShapeDtypeStruct((rows, HEAD_DIM), BF16)] * Y,
        in_specs=[vm] * (Y + count),
        out_specs=[vm] * Y,
        compiler_params=PARAMS,
        name="prefix_attention_%d" % first,
    )(*queries, *caches)


PIECE = LOCAL * HELD * (ROWS + 1)


def unpack_kernel(place_ref, line_ref, *refs):
    early, late = refs[:Y], refs[Y : 2 * Y]
    own_ref, other_ref, all_ref = refs[2 * Y :]
    for s in range(Y):
        base = s * OUT_ROWS
        cut = EARLY * HELD * BLOCK
        all_ref[base : base + cut, :] = early[s][:cut, :]
        all_ref[base + cut : base + OUT_ROWS, :] = late[s][: OUT_ROWS - cut, :]
    sources = jnp.concatenate(
        [ref[EARLY * HELD * BLOCK :, :] for ref in early]
        + [ref[(OWNED - EARLY) * HELD * BLOCK :, :] for ref in late],
        axis=0,
    )
    half = COLUMN // CORES
    size = LOCAL * HELD
    for i in range(COLUMN):
        out_ref = own_ref if i < half else other_ref
        base = (i % half) // LOCAL * PIECE
        for h in range(HELD):
            rows = pl.ds(pl.multiple_of((place_ref[i] + h * PER_GROUP) * ROWS, ROWS), ROWS)
            at = base + ((i % LOCAL) * HELD + h) * ROWS
            out_ref[at : at + ROWS, :] = all_ref[rows, :]
    wanted = line_ref[...] == iota((COLUMN * HELD, sources.shape[0]), 1)
    lines = jnp.dot(wanted.astype(BF16), sources, preferred_element_type=F32).astype(BF16)
    for i, out_ref in enumerate((own_ref, other_ref)):
        for x in range(X):
            at = (i * X + x) * size
            out_ref[x * PIECE + size * ROWS : (x + 1) * PIECE, :] = lines[at : at + size]


def unpack(place, line, parts):
    vm = pl.BlockSpec(memory_space=pltpu.VMEM)
    return pl.pallas_call(
        unpack_kernel,
        out_shape=[jax.ShapeDtypeStruct((X * PIECE, HEAD_DIM), BF16)] * CORES,
        in_specs=[pl.BlockSpec(memory_space=pltpu.SMEM)] + [vm] * (1 + 2 * Y),
        out_specs=[vm] * CORES,
        scratch_shapes=[pltpu.VMEM((Y * OUT_ROWS, HEAD_DIM), BF16)],
        compiler_params=PARAMS,
        name="unpack_results",
    )(place, line, *parts)


def merge_kernel(ours_ref, own_ref, got_ref, *out_refs):
    wide = HELD * ROWS
    for x in range(X):
        for r in range(LOCAL):
            rows = slice(x * PIECE + r * wide, x * PIECE + (r + 1) * wide)
            mine = ours_ref[x * LOCAL + r] == 1
            out_refs[x][r * wide : (r + 1) * wide, :] = jnp.where(
                mine, own_ref[rows, :], got_ref[rows, :]
            )
        rows = slice(x * PIECE + LOCAL * wide, (x + 1) * PIECE)
        out_refs[x][LOCAL * wide :, :] = own_ref[rows, :] + got_ref[rows, :]


def merge(ours, own, got):
    vm = pl.BlockSpec(memory_space=pltpu.VMEM)
    return pl.pallas_call(
        merge_kernel,
        out_shape=[jax.ShapeDtypeStruct((PIECE, HEAD_DIM), BF16)] * X,
        in_specs=[pl.BlockSpec(memory_space=pltpu.SMEM), vm, vm],
        out_specs=[vm] * X,
        compiler_params=PARAMS,
        name="merge_cores",
    )(ours, own, got)


def combine_kernel(x_ref, *refs):
    parts, (local_ref, stat_ref, out_ref, weight_ref) = refs[:X], refs[X:]
    wide = HELD * ROWS
    lane_head = iota((LOCAL, HEAD_DIM), 1) // ROWS
    heads = [lax.rem(x_ref[0] + (X - s), X) * HELD for s in range(X)]
    log_total = jnp.zeros((LOCAL, HEAD_DIM), F32)
    for s in range(X):
        pieces = parts[s][LOCAL * wide :, :].astype(F32)
        lines = pieces + pltpu.roll(pieces, HEAD_DIM - ROWS, 1)
        lines = lines + pltpu.roll(pieces, HEAD_DIM - 2 * ROWS, 1)
        for h in range(HELD):
            head = heads[s] + h
            line = pltpu.roll(lines[h * LOCAL : (h + 1) * LOCAL], head * ROWS, 1)
            log_total = jnp.where(lane_head == head, line, log_total)
    local_max = stat_ref[:LOCAL, :]
    highest = jnp.maximum(log_total, local_max)
    prefix_part = jnp.exp(log_total - highest)
    local_part = jnp.exp(local_max - highest)
    whole = prefix_part + local_part * stat_ref[LOCAL:, :]
    blank = jnp.zeros((HEAD_DIM - 2 * LOCAL, HEAD_DIM), F32)
    weight_ref[...] = jnp.concatenate([prefix_part / whole, local_part / whole, blank], axis=0).T
    for s in range(X):
        rows = pl.ds(pl.multiple_of(heads[s] * ROWS, wide), wide)
        weights = weight_ref[rows, :]
        for r in range(LOCAL):
            prefix = parts[s][r * wide : (r + 1) * wide, :].astype(F32)
            out = weights[:, r : r + 1] * prefix
            out = out + weights[:, LOCAL + r : LOCAL + r + 1] * local_ref[r, rows, :]
            out_ref[r, rows, :] = out.astype(BF16)


def combine(x, parts, local_out, stats):
    vm = pl.BlockSpec(memory_space=pltpu.VMEM)
    return pl.pallas_call(
        combine_kernel,
        out_shape=jax.ShapeDtypeStruct((LOCAL, HEADS * STEPS, HEAD_DIM), BF16),
        in_specs=[pl.BlockSpec(memory_space=pltpu.SMEM)] + [vm] * (X + 2),
        out_specs=vm,
        scratch_shapes=[pltpu.VMEM((HEAD_DIM, HEAD_DIM), F32)],
        compiler_params=PARAMS,
        name="combine_parts",
    )(x, *parts, local_out, stats)


def turn_x(value, turns):
    return lax.ppermute(value, "x", [(i, (i + turns) % X) for i in range(X)])


def shift(value, turns):
    return lax.ppermute(value, "y", [(i, (i + turns) % Y) for i in range(Y)])


def swap_cores(value):
    return lax.ppermute(value, "core", [(i, 1 - i) for i in range(CORES)])


def onward(value):
    pairs = []
    for z in range(Z):
        pairs.append((z * CORES, (z + 1) % Z * CORES))
        pairs.append((z * CORES + 1, (z - 1) % Z * CORES + 1))
    return lax.ppermute(value, ("z", "core"), pairs)


def per_device(
    queries,
    new_keys,
    new_values,
    suffix_keys,
    suffix_values,
    suffix_length,
    group_ids,
    prefix_keys,
    prefix_values,
    prefix_length,
):
    z = lax.axis_index("z")
    core = lax.axis_index("core")
    x = lax.axis_index("x")
    at_x = x.reshape(1).astype(jnp.int32)

    def head_rows(value):
        heads = value.shape[2] // HEAD_DIM
        value = value.reshape(LOCAL, STEPS, heads, HEAD_DIM).transpose(0, 2, 1, 3)
        return value.reshape(LOCAL, heads * STEPS, HEAD_DIM)

    splits = split(at_x, head_rows(queries))
    mine = build_cache(prefix_length, prefix_keys, prefix_values, splits[0])
    arrived = [splits[0]] + [turn_x(splits[s], s) for s in range(1, X)]
    own_queries = stack([arrived[-s % X] for s in range(X)])

    block_ids = group_ids[:, 0]
    ids = jnp.stack([block_ids, swap_cores(block_ids)])
    ids = lax.dynamic_slice_in_dim(
        jnp.concatenate([ids, ids], axis=1), x * LOCAL, X * LOCAL, axis=1
    ).reshape(COLUMN)
    index = jnp.arange(COLUMN, dtype=jnp.int32)
    block = index // (X * LOCAL)
    same = jnp.logical_and(ids[:, None] == ids[None, :], block[:, None] == block[None, :])
    position = jnp.sum(
        jnp.logical_and(same, index[:, None] > index[None, :]), axis=1, dtype=jnp.int32
    )
    turn = ((ids // CORES) % Y - lax.axis_index("y") + Y) % Y
    owner_core = ids % CORES
    ahead = (ids // (CORES * Y) - z + Z) % Z
    half = Z // 2
    side = jnp.where(ahead % half == 0, owner_core, (ahead < half).astype(jnp.int32))
    steps = jnp.where(ahead > half, Z - ahead, ahead)
    arrival = jnp.where(steps == 0, 0, 2 * steps - (owner_core == side).astype(jnp.int32))
    slot = block * (PER_GROUP // CORES) + position
    unit = arrival * (HELD * PER_GROUP) + slot
    place = turn * (UNITS * PER_GROUP) + unit
    ours = side == core
    counts = (EARLY * HELD * PER_GROUP, (OWNED - EARLY) * HELD * PER_GROUP)
    late_line = Y * padded(counts[0]) + turn * padded(counts[1]) + unit - counts[0]
    line = jnp.where(arrival < EARLY, turn * padded(counts[0]) + unit, late_line)
    line = jnp.where(ours, line, -HELD * PER_GROUP).reshape(CORES * X, 1, LOCAL)
    line = line + jnp.arange(HELD, dtype=jnp.int32)[:, None] * PER_GROUP
    line = line.reshape(COLUMN * HELD, 1)

    own_1, other_0 = onward(mine), swap_cores(mine)
    other_queries = swap_cores(own_queries)
    own_2, other_1 = onward(own_1), onward(other_0)
    packed = pack(jnp.where(ours, place, DUMP), own_queries, other_queries)
    received = [packed[0]] + [shift(packed[s], s) for s in range(1, Y)]
    own_3, other_2 = onward(own_2), onward(other_1)
    early = attend_prefix(0, received, [mine, own_1, other_1, own_2, other_2])
    own_4, other_3 = onward(own_3), onward(other_2)
    late = attend_prefix(EARLY, received, [own_3, other_3, own_4])
    parts = []
    for results in (early, late):
        parts += [results[0]] + [shift(results[s], -s) for s in range(1, Y)]

    local_out, stats = attend_local(
        suffix_length,
        head_rows(queries),
        suffix_keys,
        suffix_values,
        head_rows(new_keys),
        head_rows(new_values),
    )
    own_back, other_back = unpack(jnp.where(ours, place, 0), line, parts)
    pieces = merge(ours.astype(jnp.int32), own_back, swap_cores(other_back))
    got = [pieces[0]] + [turn_x(pieces[s], s) for s in range(1, X)]
    out = combine(at_x, got, local_out, stats)
    out = out.reshape(LOCAL, HEADS, STEPS, HEAD_DIM).transpose(0, 2, 1, 3)
    return out.reshape(LOCAL, STEPS, HEADS * HEAD_DIM)


def solution(mesh):
    axes = ("z", "y", "core", "x")
    fine = Mesh(mesh.devices.reshape(Z, Y, CORES, X), axes)
    rows = P(axes, None, None)
    groups = ("z", "y", "core")
    placed = (rows,) * 5 + (
        P(axes),
        P(groups, None),
        P(groups, None, "x"),
        P(groups, None, "x"),
        P(groups),
    )
    return jax.shard_map(
        per_device, mesh=fine, in_specs=placed, out_specs=rows, check_vma=False
    )
```

```python
import functools
import math

import jax
import jax.numpy as jnp
from jax import lax
from jax.experimental import pallas as pl
from jax.experimental.pallas import tpu as pltpu
from jax.sharding import Mesh, PartitionSpec as P

HEADS = 64
KV_HEADS = 8
HEAD_DIM = 128
PREFIX_MAX = 256
STEPS = 2
SUFFIX_MAX = 32
GROUP = HEADS // KV_HEADS
ROWS = GROUP * STEPS
FACTOR = 1.0 / math.sqrt(HEAD_DIM)
Z, Y, CORES, X = 8, 4, 2, 4
PEERS = CORES * X
LOCAL = 8
COLUMN = PEERS * LOCAL
HELD = KV_HEADS // X
OWNED = Z
EARLY = 5
PER_GROUP = 4
BLOCK = PER_GROUP * ROWS
UNITS = OWNED * HELD
OUT_ROWS = UNITS * BLOCK
DUMP = Y * OUT_ROWS // ROWS
CACHE_ROWS = 2 * HELD * PREFIX_MAX
F32 = jnp.float32
BF16 = jnp.bfloat16
TURNS = (0, 1, 3, 2)
PARAMS = pltpu.CompilerParams(vmem_limit_bytes=32 * 1024 * 1024)


def padded(count):
    return -(-count // 16) * 16


def dot_t(a, b):
    return lax.dot_general(a, b, (((1,), (1,)), ((), ())), preferred_element_type=F32)


def iota(shape, dim):
    return lax.broadcasted_iota(jnp.int32, shape, dim)


def local_kernel(length_ref, q_ref, sk_ref, sv_ref, nk_ref, nv_ref, out_ref, stat_ref):
    width = KV_HEADS * SUFFIX_MAX
    fresh = KV_HEADS * STEPS
    row = iota((HEADS * STEPS, width), 0)
    col = iota((HEADS * STEPS, width), 1)
    same_head = row // ROWS == col // SUFFIX_MAX
    position = col % SUFFIX_MAX
    row2 = iota((HEADS * STEPS, fresh), 0)
    col2 = iota((HEADS * STEPS, fresh), 1)
    seen = jnp.logical_and(row2 // ROWS == col2 // STEPS, col2 % STEPS <= row2 % STEPS)
    lane = iota((HEADS * STEPS, HEAD_DIM), 1)
    columns = jnp.zeros((HEADS * STEPS, HEAD_DIM), F32)
    for r in range(LOCAL):
        q = q_ref[r]
        keys = jnp.concatenate(
            [sk_ref[r, :, k * HEAD_DIM : (k + 1) * HEAD_DIM] for k in range(KV_HEADS)], axis=0
        )
        values = jnp.concatenate(
            [sv_ref[r, :, k * HEAD_DIM : (k + 1) * HEAD_DIM] for k in range(KV_HEADS)], axis=0
        )
        usable = jnp.logical_and(same_head, position < length_ref[r])
        old = jnp.where(usable, dot_t(q, keys) * FACTOR, -jnp.inf)
        new = jnp.where(seen, dot_t(q, nk_ref[r]) * FACTOR, -jnp.inf)
        highest = jnp.maximum(
            jnp.max(old, axis=1, keepdims=True), jnp.max(new, axis=1, keepdims=True)
        )
        old = jnp.exp(old - highest)
        new = jnp.exp(new - highest)
        total = jnp.sum(old, axis=1, keepdims=True) + jnp.sum(new, axis=1, keepdims=True)
        out = jnp.dot(old.astype(BF16), values, preferred_element_type=F32)
        out_ref[r] = out + jnp.dot(new.astype(BF16), nv_ref[r], preferred_element_type=F32)
        columns = jnp.where(lane == r, highest, jnp.where(lane == LOCAL + r, total, columns))
    stat_ref[...] = columns.T[: 2 * LOCAL]


def attend_local(lengths, q, sk, sv, nk, nv):
    vm = pl.BlockSpec(memory_space=pltpu.VMEM)
    shape = jax.ShapeDtypeStruct((LOCAL, HEADS * STEPS, HEAD_DIM), F32)
    return pl.pallas_call(
        local_kernel,
        out_shape=(shape, jax.ShapeDtypeStruct((2 * LOCAL, HEADS * STEPS), F32)),
        in_specs=[pl.BlockSpec(memory_space=pltpu.SMEM)] + [vm] * 5,
        out_specs=(vm, vm),
        compiler_params=PARAMS,
        name="local_attention",
    )(lengths, q, sk, sv, nk, nv)


def split_kernel(x_ref, q_ref, *refs):
    out_refs, sems = refs[:X], refs[X]
    wide = HELD * ROWS
    copies = []
    for s in range(X):
        head = pl.multiple_of(lax.rem(x_ref[0] + s, X) * wide, wide)
        for r in range(LOCAL):
            copies.append(
                pltpu.make_async_copy(
                    q_ref.at[r, pl.ds(head, wide), :],
                    out_refs[s].at[pl.ds(r * wide, wide), :],
                    sems.at[s, r],
                )
            )
    for copy in copies:
        copy.start()
    for copy in copies:
        copy.wait()


def split(x, q):
    part = jax.ShapeDtypeStruct((LOCAL * HELD * ROWS, HEAD_DIM), BF16)
    return pl.pallas_call(
        split_kernel,
        out_shape=[part] * X,
        in_specs=[pl.BlockSpec(memory_space=pltpu.SMEM), pl.BlockSpec(memory_space=pl.ANY)],
        out_specs=[pl.BlockSpec(memory_space=pltpu.VMEM)] * X,
        scratch_shapes=[pltpu.SemaphoreType.DMA((X, LOCAL))],
        compiler_params=PARAMS,
        name="split_queries",
    )(x, q)


def cache_kernel(length_ref, k_ref, v_ref, after_ref, cache_ref, sems):
    copies = []
    for i, ref in enumerate((k_ref, v_ref)):
        for h in range(HELD):
            at = (i * HELD + h) * PREFIX_MAX
            copies.append(
                pltpu.make_async_copy(
                    ref.at[0, :, pl.ds(h * HEAD_DIM, HEAD_DIM)],
                    cache_ref.at[pl.ds(at, PREFIX_MAX), :],
                    sems.at[i, h],
                )
            )
    for copy in copies:
        copy.start()
    length = jnp.full((16, HEAD_DIM), length_ref[0], jnp.int32)
    cache_ref[CACHE_ROWS:, :] = length.astype(F32).astype(BF16)
    for copy in copies:
        copy.wait()


def build_cache(length, keys, values, after):
    anywhere = pl.BlockSpec(memory_space=pl.ANY)
    return pl.pallas_call(
        cache_kernel,
        out_shape=jax.ShapeDtypeStruct((CACHE_ROWS + 16, HEAD_DIM), BF16),
        in_specs=[pl.BlockSpec(memory_space=pltpu.SMEM)] + [anywhere] * 3,
        out_specs=pl.BlockSpec(memory_space=pltpu.VMEM),
        scratch_shapes=[pltpu.SemaphoreType.DMA((2, HELD))],
        compiler_params=PARAMS,
        name="build_cache",
    )(length, keys, values, after)


def stack_kernel(*refs):
    parts, out_ref = refs[:-1], refs[-1]
    size = parts[0].shape[0]
    for i, ref in enumerate(parts):
        out_ref[i * size : (i + 1) * size, :] = ref[...]


def stack(parts):
    vm = pl.BlockSpec(memory_space=pltpu.VMEM)
    size, width = parts[0].shape
    return pl.pallas_call(
        stack_kernel,
        out_shape=jax.ShapeDtypeStruct((len(parts) * size, width), parts[0].dtype),
        in_specs=[vm] * len(parts),
        out_specs=vm,
        compiler_params=PARAMS,
        name="stack_queries",
    )(*parts)


def pack_kernel(place_ref, own_ref, other_ref, *out_refs):
    packed_ref = out_refs[Y]
    packed_ref[...] = jnp.zeros(packed_ref.shape, BF16)
    half = COLUMN // CORES
    for i in range(COLUMN):
        q_ref = own_ref if i < half else other_ref
        for h in range(HELD):
            start = pl.multiple_of((place_ref[i] + h * PER_GROUP) * ROWS, ROWS)
            at = ((i % half) * HELD + h) * ROWS
            packed_ref[pl.ds(start, ROWS), :] = q_ref[at : at + ROWS, :]
    for s in range(Y):
        out_refs[s][...] = packed_ref[s * OUT_ROWS : (s + 1) * OUT_ROWS, :]


def pack(place, own, other):
    vm = pl.BlockSpec(memory_space=pltpu.VMEM)
    return pl.pallas_call(
        pack_kernel,
        out_shape=[jax.ShapeDtypeStruct((OUT_ROWS, HEAD_DIM), BF16)] * Y,
        in_specs=[pl.BlockSpec(memory_space=pltpu.SMEM), vm, vm],
        out_specs=[vm] * Y,
        scratch_shapes=[pltpu.VMEM((Y * OUT_ROWS + 2 * BLOCK, HEAD_DIM), BF16)],
        compiler_params=PARAMS,
        name="pack_queries",
    )(place, own, other)


def prefix_kernel(first, count, *refs):
    q_refs, caches, out_refs = refs[:Y], refs[Y : Y + count], refs[Y + count :]
    column = iota((1, PREFIX_MAX), 1).astype(F32)
    lane = iota((Y * BLOCK, HEAD_DIM), 1)
    diagonal = lane % ROWS == iota((Y * BLOCK, HEAD_DIM), 0) % ROWS
    piece = iota((Y * PER_GROUP, HEAD_DIM), 1) // ROWS
    lines = []
    for j in range(count):
        length = caches[j][CACHE_ROWS:, :].astype(F32)[:1, :1]
        usable = column < length
        for h in range(HELD):
            unit = (first + j) * HELD + h
            q = jnp.concatenate(
                [ref[unit * BLOCK : (unit + 1) * BLOCK, :] for ref in q_refs], axis=0
            )
            keys = caches[j][h * PREFIX_MAX : (h + 1) * PREFIX_MAX, :]
            values = caches[j][(HELD + h) * PREFIX_MAX : (HELD + h + 1) * PREFIX_MAX, :]
            scores = jnp.where(usable, dot_t(q, keys) * FACTOR, -jnp.inf)
            highest = jnp.max(scores, axis=1, keepdims=True)
            weights = jnp.exp(scores - highest)
            total = jnp.sum(weights, axis=1, keepdims=True)
            out = jnp.dot(weights.astype(BF16), values, preferred_element_type=F32)
            out = (out / total).astype(BF16)
            at = (j * HELD + h) * BLOCK
            for s in range(Y):
                out_refs[s][at : at + BLOCK, :] = out[s * BLOCK : (s + 1) * BLOCK]
            log_total = jnp.where(diagonal, highest + jnp.log(total), 0.0)
            line = jnp.sum(log_total.reshape(Y * PER_GROUP, ROWS, HEAD_DIM), axis=1)
            upper = line.astype(BF16).astype(F32)
            remain = line - upper
            middle = remain.astype(BF16).astype(F32)
            lowest = remain - middle
            lines.append(jnp.where(piece == 0, upper, jnp.where(piece == 1, middle, lowest)))
    units = count * HELD
    blank = padded(units * PER_GROUP) - units * PER_GROUP
    for s in range(Y):
        part = [x[s * PER_GROUP : (s + 1) * PER_GROUP] for x in lines]
        if blank:
            part.append(jnp.zeros((blank, HEAD_DIM), F32))
        out_refs[s][units * BLOCK :, :] = jnp.concatenate(part, axis=0).astype(BF16)


def attend_prefix(first, queries, caches):
    count = len(caches)
    units = count * HELD
    rows = units * BLOCK + padded(units * PER_GROUP)
    vm = pl.BlockSpec(memory_space=pltpu.VMEM)
    return pl.pallas_call(
        functools.partial(prefix_kernel, first, count),
        out_shape=[jax.ShapeDtypeStruct((rows, HEAD_DIM), BF16)] * Y,
        in_specs=[vm] * (Y + count),
        out_specs=[vm] * Y,
        compiler_params=PARAMS,
        name="prefix_attention_%d" % first,
    )(*queries, *caches)


PIECE = LOCAL * HELD * (ROWS + 1)


def unpack_kernel(place_ref, line_ref, *refs):
    early, late = refs[:Y], refs[Y : 2 * Y]
    own_ref, other_ref, all_ref = refs[2 * Y :]
    for s in range(Y):
        base = s * OUT_ROWS
        cut = EARLY * HELD * BLOCK
        all_ref[base : base + cut, :] = early[s][:cut, :]
        all_ref[base + cut : base + OUT_ROWS, :] = late[s][: OUT_ROWS - cut, :]
    sources = jnp.concatenate(
        [ref[EARLY * HELD * BLOCK :, :] for ref in early]
        + [ref[(OWNED - EARLY) * HELD * BLOCK :, :] for ref in late],
        axis=0,
    )
    half = COLUMN // CORES
    size = LOCAL * HELD
    for i in range(COLUMN):
        out_ref = own_ref if i < half else other_ref
        base = (i % half) // LOCAL * PIECE
        for h in range(HELD):
            rows = pl.ds(pl.multiple_of((place_ref[i] + h * PER_GROUP) * ROWS, ROWS), ROWS)
            at = base + ((i % LOCAL) * HELD + h) * ROWS
            out_ref[at : at + ROWS, :] = all_ref[rows, :]
    wanted = line_ref[...] == iota((COLUMN * HELD, sources.shape[0]), 1)
    lines = jnp.dot(wanted.astype(BF16), sources, preferred_element_type=F32).astype(BF16)
    for i, out_ref in enumerate((own_ref, other_ref)):
        for x in range(X):
            at = (i * X + x) * size
            out_ref[x * PIECE + size * ROWS : (x + 1) * PIECE, :] = lines[at : at + size]


def unpack(place, line, parts):
    vm = pl.BlockSpec(memory_space=pltpu.VMEM)
    return pl.pallas_call(
        unpack_kernel,
        out_shape=[jax.ShapeDtypeStruct((X * PIECE, HEAD_DIM), BF16)] * CORES,
        in_specs=[pl.BlockSpec(memory_space=pltpu.SMEM)] + [vm] * (1 + 2 * Y),
        out_specs=[vm] * CORES,
        scratch_shapes=[pltpu.VMEM((Y * OUT_ROWS, HEAD_DIM), BF16)],
        compiler_params=PARAMS,
        name="unpack_results",
    )(place, line, *parts)


def merge_kernel(ours_ref, own_ref, got_ref, *out_refs):
    wide = HELD * ROWS
    for x in range(X):
        for r in range(LOCAL):
            rows = slice(x * PIECE + r * wide, x * PIECE + (r + 1) * wide)
            mine = ours_ref[x * LOCAL + r] == 1
            out_refs[x][r * wide : (r + 1) * wide, :] = jnp.where(
                mine, own_ref[rows, :], got_ref[rows, :]
            )
        rows = slice(x * PIECE + LOCAL * wide, (x + 1) * PIECE)
        out_refs[x][LOCAL * wide :, :] = own_ref[rows, :] + got_ref[rows, :]


def merge(ours, own, got):
    vm = pl.BlockSpec(memory_space=pltpu.VMEM)
    return pl.pallas_call(
        merge_kernel,
        out_shape=[jax.ShapeDtypeStruct((PIECE, HEAD_DIM), BF16)] * X,
        in_specs=[pl.BlockSpec(memory_space=pltpu.SMEM), vm, vm],
        out_specs=[vm] * X,
        compiler_params=PARAMS,
        name="merge_cores",
    )(ours, own, got)


def combine_kernel(x_ref, *refs):
    parts, (local_ref, stat_ref, out_ref, weight_ref) = refs[:X], refs[X:]
    wide = HELD * ROWS
    lane_head = iota((LOCAL, HEAD_DIM), 1) // ROWS
    heads = [lax.rem(x_ref[0] + (X - s), X) * HELD for s in range(X)]
    log_total = jnp.zeros((LOCAL, HEAD_DIM), F32)
    for s in range(X):
        pieces = parts[s][LOCAL * wide :, :].astype(F32)
        lines = pieces + pltpu.roll(pieces, HEAD_DIM - ROWS, 1)
        lines = lines + pltpu.roll(pieces, HEAD_DIM - 2 * ROWS, 1)
        for h in range(HELD):
            head = heads[s] + h
            line = pltpu.roll(lines[h * LOCAL : (h + 1) * LOCAL], head * ROWS, 1)
            log_total = jnp.where(lane_head == head, line, log_total)
    local_max = stat_ref[:LOCAL, :]
    highest = jnp.maximum(log_total, local_max)
    prefix_part = jnp.exp(log_total - highest)
    local_part = jnp.exp(local_max - highest)
    whole = prefix_part + local_part * stat_ref[LOCAL:, :]
    blank = jnp.zeros((HEAD_DIM - 2 * LOCAL, HEAD_DIM), F32)
    weight_ref[...] = jnp.concatenate([prefix_part / whole, local_part / whole, blank], axis=0).T
    for s in range(X):
        rows = pl.ds(pl.multiple_of(heads[s] * ROWS, wide), wide)
        weights = weight_ref[rows, :]
        for r in range(LOCAL):
            prefix = parts[s][r * wide : (r + 1) * wide, :].astype(F32)
            out = weights[:, r : r + 1] * prefix
            out = out + weights[:, LOCAL + r : LOCAL + r + 1] * local_ref[r, rows, :]
            out_ref[r, rows, :] = out.astype(BF16)


def combine(x, parts, local_out, stats):
    vm = pl.BlockSpec(memory_space=pltpu.VMEM)
    return pl.pallas_call(
        combine_kernel,
        out_shape=jax.ShapeDtypeStruct((LOCAL, HEADS * STEPS, HEAD_DIM), BF16),
        in_specs=[pl.BlockSpec(memory_space=pltpu.SMEM)] + [vm] * (X + 2),
        out_specs=vm,
        scratch_shapes=[pltpu.VMEM((HEAD_DIM, HEAD_DIM), F32)],
        compiler_params=PARAMS,
        name="combine_parts",
    )(x, *parts, local_out, stats)


def turn_x(value, turns):
    return lax.ppermute(value, "x", [(i, (i + turns) % X) for i in range(X)])


def shift(value, turns):
    return lax.ppermute(value, "y", [(i, (i + turns) % Y) for i in range(Y)])


def swap_cores(value):
    return lax.ppermute(value, "core", [(i, 1 - i) for i in range(CORES)])


def onward(value):
    pairs = []
    for z in range(Z):
        pairs.append((z * CORES, (z + 1) % Z * CORES))
        pairs.append((z * CORES + 1, (z - 1) % Z * CORES + 1))
    return lax.ppermute(value, ("z", "core"), pairs)


def per_device(
    queries,
    new_keys,
    new_values,
    suffix_keys,
    suffix_values,
    suffix_length,
    group_ids,
    prefix_keys,
    prefix_values,
    prefix_length,
):
    z = lax.axis_index("z")
    core = lax.axis_index("core")
    x = lax.axis_index("x")
    at_x = x.reshape(1).astype(jnp.int32)

    def head_rows(value):
        heads = value.shape[2] // HEAD_DIM
        value = value.reshape(LOCAL, STEPS, heads, HEAD_DIM).transpose(0, 2, 1, 3)
        return value.reshape(LOCAL, heads * STEPS, HEAD_DIM)

    splits = split(at_x, head_rows(queries))
    mine = build_cache(prefix_length, prefix_keys, prefix_values, splits[0])
    arrived = [splits[0]] + [turn_x(splits[s], s) for s in range(1, X)]
    own_queries = stack([arrived[-s % X] for s in range(X)])

    block_ids = group_ids[:, 0]
    ids = jnp.stack([block_ids, swap_cores(block_ids)])
    ids = lax.dynamic_slice_in_dim(
        jnp.concatenate([ids, ids], axis=1), x * LOCAL, X * LOCAL, axis=1
    ).reshape(COLUMN)
    index = jnp.arange(COLUMN, dtype=jnp.int32)
    block = index // (X * LOCAL)
    same = jnp.logical_and(ids[:, None] == ids[None, :], block[:, None] == block[None, :])
    position = jnp.sum(
        jnp.logical_and(same, index[:, None] > index[None, :]), axis=1, dtype=jnp.int32
    )
    turn = ((ids // CORES) % Y - lax.axis_index("y") + Y) % Y
    turn = jnp.where(turn < 2, turn, Y + 1 - turn)
    owner_core = ids % CORES
    ahead = (ids // (CORES * Y) - z + Z) % Z
    half = Z // 2
    side = jnp.where(ahead % half == 0, owner_core, (ahead < half).astype(jnp.int32))
    steps = jnp.where(ahead > half, Z - ahead, ahead)
    arrival = jnp.where(steps == 0, 0, 2 * steps - (owner_core == side).astype(jnp.int32))
    slot = block * (PER_GROUP // CORES) + position
    unit = arrival * (HELD * PER_GROUP) + slot
    place = turn * (UNITS * PER_GROUP) + unit
    ours = side == core
    counts = (EARLY * HELD * PER_GROUP, (OWNED - EARLY) * HELD * PER_GROUP)
    late_line = Y * padded(counts[0]) + turn * padded(counts[1]) + unit - counts[0]
    line = jnp.where(arrival < EARLY, turn * padded(counts[0]) + unit, late_line)
    line = jnp.where(ours, line, -HELD * PER_GROUP).reshape(CORES * X, 1, LOCAL)
    line = line + jnp.arange(HELD, dtype=jnp.int32)[:, None] * PER_GROUP
    line = line.reshape(COLUMN * HELD, 1)

    own_1, other_0 = onward(mine), swap_cores(mine)
    other_queries = swap_cores(own_queries)
    own_2, other_1 = onward(own_1), onward(other_0)
    packed = pack(jnp.where(ours, place, DUMP), own_queries, other_queries)
    received = [packed[0]] + [shift(packed[s], TURNS[s]) for s in range(1, Y)]
    own_3, other_2 = onward(own_2), onward(other_1)
    early = attend_prefix(0, received, [mine, own_1, other_1, own_2, other_2])
    own_4, other_3 = onward(own_3), onward(other_2)
    late = attend_prefix(EARLY, received, [own_3, other_3, own_4])
    parts = []
    for results in (early, late):
        parts += [results[0]] + [shift(results[s], -TURNS[s]) for s in range(1, Y)]

    local_out, stats = attend_local(
        suffix_length,
        head_rows(queries),
        suffix_keys,
        suffix_values,
        head_rows(new_keys),
        head_rows(new_values),
    )
    own_back, other_back = unpack(jnp.where(ours, place, 0), line, parts)
    pieces = merge(ours.astype(jnp.int32), own_back, swap_cores(other_back))
    got = [pieces[0]] + [turn_x(pieces[s], s) for s in range(1, X)]
    out = combine(at_x, got, local_out, stats)
    out = out.reshape(LOCAL, HEADS, STEPS, HEAD_DIM).transpose(0, 2, 1, 3)
    return out.reshape(LOCAL, STEPS, HEADS * HEAD_DIM)


def solution(mesh):
    axes = ("z", "y", "core", "x")
    fine = Mesh(mesh.devices.reshape(Z, Y, CORES, X), axes)
    rows = P(axes, None, None)
    groups = ("z", "y", "core")
    placed = (rows,) * 5 + (
        P(axes),
        P(groups, None),
        P(groups, None, "x"),
        P(groups, None, "x"),
        P(groups),
    )
    return jax.shard_map(
        per_device, mesh=fine, in_specs=placed, out_specs=rows, check_vma=False
    )
```

```python
import functools
import math

import jax
import jax.numpy as jnp
from jax import lax
from jax.experimental import pallas as pl
from jax.experimental.pallas import tpu as pltpu
from jax.sharding import Mesh, PartitionSpec as P

HEADS = 64
KV_HEADS = 8
HEAD_DIM = 128
PREFIX_MAX = 256
STEPS = 2
SUFFIX_MAX = 32
GROUP = HEADS // KV_HEADS
ROWS = GROUP * STEPS
FACTOR = 1.0 / math.sqrt(HEAD_DIM)
Z, Y, CORES, X = 8, 4, 2, 4
PEERS = CORES * X
LOCAL = 8
COLUMN = PEERS * LOCAL
HELD = KV_HEADS // X
OWNED = Z
EARLY = 5
PER_GROUP = 4
BLOCK = PER_GROUP * ROWS
UNITS = OWNED * HELD
OUT_ROWS = UNITS * BLOCK
DUMP = Y * OUT_ROWS // ROWS
CACHE_ROWS = 2 * HELD * PREFIX_MAX
F32 = jnp.float32
BF16 = jnp.bfloat16
TURNS = (0, 1, 3, 2)
PARAMS = pltpu.CompilerParams(vmem_limit_bytes=32 * 1024 * 1024)


def padded(count):
    return -(-count // 16) * 16


def dot_t(a, b):
    return lax.dot_general(a, b, (((1,), (1,)), ((), ())), preferred_element_type=F32)


def iota(shape, dim):
    return lax.broadcasted_iota(jnp.int32, shape, dim)


def local_kernel(length_ref, q_ref, sk_ref, sv_ref, nk_ref, nv_ref, out_ref, stat_ref):
    width = KV_HEADS * SUFFIX_MAX
    fresh = KV_HEADS * STEPS
    row = iota((HEADS * STEPS, width), 0)
    col = iota((HEADS * STEPS, width), 1)
    same_head = row // ROWS == col // SUFFIX_MAX
    position = col % SUFFIX_MAX
    row2 = iota((HEADS * STEPS, fresh), 0)
    col2 = iota((HEADS * STEPS, fresh), 1)
    seen = jnp.logical_and(row2 // ROWS == col2 // STEPS, col2 % STEPS <= row2 % STEPS)
    lane = iota((HEADS * STEPS, HEAD_DIM), 1)
    columns = jnp.zeros((HEADS * STEPS, HEAD_DIM), F32)
    for r in range(LOCAL):
        q = q_ref[r]
        keys = jnp.concatenate(
            [sk_ref[r, :, k * HEAD_DIM : (k + 1) * HEAD_DIM] for k in range(KV_HEADS)], axis=0
        )
        values = jnp.concatenate(
            [sv_ref[r, :, k * HEAD_DIM : (k + 1) * HEAD_DIM] for k in range(KV_HEADS)], axis=0
        )
        usable = jnp.logical_and(same_head, position < length_ref[r])
        old = jnp.where(usable, dot_t(q, keys) * FACTOR, -jnp.inf)
        new = jnp.where(seen, dot_t(q, nk_ref[r]) * FACTOR, -jnp.inf)
        highest = jnp.maximum(
            jnp.max(old, axis=1, keepdims=True), jnp.max(new, axis=1, keepdims=True)
        )
        old = jnp.exp(old - highest)
        new = jnp.exp(new - highest)
        total = jnp.sum(old, axis=1, keepdims=True) + jnp.sum(new, axis=1, keepdims=True)
        out = jnp.dot(old.astype(BF16), values, preferred_element_type=F32)
        out_ref[r] = out + jnp.dot(new.astype(BF16), nv_ref[r], preferred_element_type=F32)
        columns = jnp.where(lane == r, highest, jnp.where(lane == LOCAL + r, total, columns))
    stat_ref[...] = columns.T[: 2 * LOCAL]


def attend_local(lengths, q, sk, sv, nk, nv):
    vm = pl.BlockSpec(memory_space=pltpu.VMEM)
    shape = jax.ShapeDtypeStruct((LOCAL, HEADS * STEPS, HEAD_DIM), F32)
    return pl.pallas_call(
        local_kernel,
        out_shape=(shape, jax.ShapeDtypeStruct((2 * LOCAL, HEADS * STEPS), F32)),
        in_specs=[pl.BlockSpec(memory_space=pltpu.SMEM)] + [vm] * 5,
        out_specs=(vm, vm),
        compiler_params=PARAMS,
        name="local_attention",
    )(lengths, q, sk, sv, nk, nv)


def split_kernel(x_ref, q_ref, *out_refs):
    wide = HELD * ROWS
    for s in range(X):
        head = pl.multiple_of(lax.rem(x_ref[0] + s, X) * wide, wide)
        for r in range(LOCAL):
            out_refs[s][r * wide : (r + 1) * wide, :] = q_ref[r, pl.ds(head, wide), :]


def split(x, q):
    vm = pl.BlockSpec(memory_space=pltpu.VMEM)
    part = jax.ShapeDtypeStruct((LOCAL * HELD * ROWS, HEAD_DIM), BF16)
    return pl.pallas_call(
        split_kernel,
        out_shape=[part] * X,
        in_specs=[pl.BlockSpec(memory_space=pltpu.SMEM), vm],
        out_specs=[vm] * X,
        compiler_params=PARAMS,
        name="split_queries",
    )(x, q)


def cache_kernel(length_ref, k_ref, v_ref, after_ref, cache_ref, sems):
    copies = []
    for i, ref in enumerate((k_ref, v_ref)):
        for h in range(HELD):
            at = (i * HELD + h) * PREFIX_MAX
            copies.append(
                pltpu.make_async_copy(
                    ref.at[0, :, pl.ds(h * HEAD_DIM, HEAD_DIM)],
                    cache_ref.at[pl.ds(at, PREFIX_MAX), :],
                    sems.at[i, h],
                )
            )
    for copy in copies:
        copy.start()
    length = jnp.full((16, HEAD_DIM), length_ref[0], jnp.int32)
    cache_ref[CACHE_ROWS:, :] = length.astype(F32).astype(BF16)
    for copy in copies:
        copy.wait()


def build_cache(length, keys, values, after):
    anywhere = pl.BlockSpec(memory_space=pl.ANY)
    return pl.pallas_call(
        cache_kernel,
        out_shape=jax.ShapeDtypeStruct((CACHE_ROWS + 16, HEAD_DIM), BF16),
        in_specs=[pl.BlockSpec(memory_space=pltpu.SMEM)] + [anywhere] * 3,
        out_specs=pl.BlockSpec(memory_space=pltpu.VMEM),
        scratch_shapes=[pltpu.SemaphoreType.DMA((2, HELD))],
        compiler_params=PARAMS,
        name="build_cache",
    )(length, keys, values, after)


def stack_kernel(*refs):
    parts, out_ref = refs[:-1], refs[-1]
    size = parts[0].shape[0]
    for turn, ref in zip(TURNS, parts):
        i = -turn % X
        out_ref[i * size : (i + 1) * size, :] = ref[...]


def stack(parts):
    vm = pl.BlockSpec(memory_space=pltpu.VMEM)
    size, width = parts[0].shape
    return pl.pallas_call(
        stack_kernel,
        out_shape=jax.ShapeDtypeStruct((len(parts) * size, width), parts[0].dtype),
        in_specs=[vm] * len(parts),
        out_specs=vm,
        compiler_params=PARAMS,
        name="stack_queries",
    )(*parts)


def pack_kernel(place_ref, own_ref, other_ref, *out_refs):
    packed_ref = out_refs[Y]
    packed_ref[...] = jnp.zeros(packed_ref.shape, BF16)
    half = COLUMN // CORES
    for i in range(COLUMN):
        q_ref = own_ref if i < half else other_ref
        for h in range(HELD):
            start = pl.multiple_of((place_ref[i] + h * PER_GROUP) * ROWS, ROWS)
            at = ((i % half) * HELD + h) * ROWS
            packed_ref[pl.ds(start, ROWS), :] = q_ref[at : at + ROWS, :]
    for s in range(Y):
        out_refs[s][...] = packed_ref[s * OUT_ROWS : (s + 1) * OUT_ROWS, :]


def pack(place, own, other):
    vm = pl.BlockSpec(memory_space=pltpu.VMEM)
    return pl.pallas_call(
        pack_kernel,
        out_shape=[jax.ShapeDtypeStruct((OUT_ROWS, HEAD_DIM), BF16)] * Y,
        in_specs=[pl.BlockSpec(memory_space=pltpu.SMEM), vm, vm],
        out_specs=[vm] * Y,
        scratch_shapes=[pltpu.VMEM((Y * OUT_ROWS + 2 * BLOCK, HEAD_DIM), BF16)],
        compiler_params=PARAMS,
        name="pack_queries",
    )(place, own, other)


def prefix_kernel(first, count, *refs):
    q_refs, caches, out_refs = refs[:Y], refs[Y : Y + count], refs[Y + count :]
    column = iota((1, PREFIX_MAX), 1).astype(F32)
    lane = iota((Y * BLOCK, HEAD_DIM), 1)
    diagonal = lane % ROWS == iota((Y * BLOCK, HEAD_DIM), 0) % ROWS
    piece = iota((Y * PER_GROUP, HEAD_DIM), 1) // ROWS
    lines = []
    for j in range(count):
        length = caches[j][CACHE_ROWS:, :].astype(F32)[:1, :1]
        usable = column < length
        for h in range(HELD):
            unit = (first + j) * HELD + h
            q = jnp.concatenate(
                [ref[unit * BLOCK : (unit + 1) * BLOCK, :] for ref in q_refs], axis=0
            )
            keys = caches[j][h * PREFIX_MAX : (h + 1) * PREFIX_MAX, :]
            values = caches[j][(HELD + h) * PREFIX_MAX : (HELD + h + 1) * PREFIX_MAX, :]
            scores = jnp.where(usable, dot_t(q, keys) * FACTOR, -jnp.inf)
            highest = jnp.max(scores, axis=1, keepdims=True)
            weights = jnp.exp(scores - highest)
            total = jnp.sum(weights, axis=1, keepdims=True)
            out = jnp.dot(weights.astype(BF16), values, preferred_element_type=F32)
            out = (out / total).astype(BF16)
            at = (j * HELD + h) * BLOCK
            for s in range(Y):
                out_refs[s][at : at + BLOCK, :] = out[s * BLOCK : (s + 1) * BLOCK]
            log_total = jnp.where(diagonal, highest + jnp.log(total), 0.0)
            line = jnp.sum(log_total.reshape(Y * PER_GROUP, ROWS, HEAD_DIM), axis=1)
            upper = line.astype(BF16).astype(F32)
            remain = line - upper
            middle = remain.astype(BF16).astype(F32)
            lowest = remain - middle
            lines.append(jnp.where(piece == 0, upper, jnp.where(piece == 1, middle, lowest)))
    units = count * HELD
    blank = padded(units * PER_GROUP) - units * PER_GROUP
    for s in range(Y):
        part = [x[s * PER_GROUP : (s + 1) * PER_GROUP] for x in lines]
        if blank:
            part.append(jnp.zeros((blank, HEAD_DIM), F32))
        out_refs[s][units * BLOCK :, :] = jnp.concatenate(part, axis=0).astype(BF16)


def attend_prefix(first, queries, caches):
    count = len(caches)
    units = count * HELD
    rows = units * BLOCK + padded(units * PER_GROUP)
    vm = pl.BlockSpec(memory_space=pltpu.VMEM)
    return pl.pallas_call(
        functools.partial(prefix_kernel, first, count),
        out_shape=[jax.ShapeDtypeStruct((rows, HEAD_DIM), BF16)] * Y,
        in_specs=[vm] * (Y + count),
        out_specs=[vm] * Y,
        compiler_params=PARAMS,
        name="prefix_attention_%d" % first,
    )(*queries, *caches)


PIECE = LOCAL * HELD * (ROWS + 1)


def unpack_kernel(place_ref, line_ref, *refs):
    early, late = refs[:Y], refs[Y : 2 * Y]
    own_ref, other_ref, all_ref = refs[2 * Y :]
    for s in range(Y):
        base = s * OUT_ROWS
        cut = EARLY * HELD * BLOCK
        all_ref[base : base + cut, :] = early[s][:cut, :]
        all_ref[base + cut : base + OUT_ROWS, :] = late[s][: OUT_ROWS - cut, :]
    sources = jnp.concatenate(
        [ref[EARLY * HELD * BLOCK :, :] for ref in early]
        + [ref[(OWNED - EARLY) * HELD * BLOCK :, :] for ref in late],
        axis=0,
    )
    half = COLUMN // CORES
    size = LOCAL * HELD
    for i in range(COLUMN):
        out_ref = own_ref if i < half else other_ref
        base = (i % half) // LOCAL * PIECE
        for h in range(HELD):
            rows = pl.ds(pl.multiple_of((place_ref[i] + h * PER_GROUP) * ROWS, ROWS), ROWS)
            at = base + ((i % LOCAL) * HELD + h) * ROWS
            out_ref[at : at + ROWS, :] = all_ref[rows, :]
    wanted = line_ref[...] == iota((COLUMN * HELD, sources.shape[0]), 1)
    lines = jnp.dot(wanted.astype(BF16), sources, preferred_element_type=F32).astype(BF16)
    for i, out_ref in enumerate((own_ref, other_ref)):
        for x in range(X):
            at = (i * X + x) * size
            out_ref[x * PIECE + size * ROWS : (x + 1) * PIECE, :] = lines[at : at + size]


def unpack(place, line, parts):
    vm = pl.BlockSpec(memory_space=pltpu.VMEM)
    return pl.pallas_call(
        unpack_kernel,
        out_shape=[jax.ShapeDtypeStruct((X * PIECE, HEAD_DIM), BF16)] * CORES,
        in_specs=[pl.BlockSpec(memory_space=pltpu.SMEM)] + [vm] * (1 + 2 * Y),
        out_specs=[vm] * CORES,
        scratch_shapes=[pltpu.VMEM((Y * OUT_ROWS, HEAD_DIM), BF16)],
        compiler_params=PARAMS,
        name="unpack_results",
    )(place, line, *parts)


def merge_kernel(ours_ref, own_ref, got_ref, *out_refs):
    wide = HELD * ROWS
    for x in range(X):
        for r in range(LOCAL):
            rows = slice(x * PIECE + r * wide, x * PIECE + (r + 1) * wide)
            mine = ours_ref[x * LOCAL + r] == 1
            out_refs[x][r * wide : (r + 1) * wide, :] = jnp.where(
                mine, own_ref[rows, :], got_ref[rows, :]
            )
        rows = slice(x * PIECE + LOCAL * wide, (x + 1) * PIECE)
        out_refs[x][LOCAL * wide :, :] = own_ref[rows, :] + got_ref[rows, :]


def merge(ours, own, got):
    vm = pl.BlockSpec(memory_space=pltpu.VMEM)
    return pl.pallas_call(
        merge_kernel,
        out_shape=[jax.ShapeDtypeStruct((PIECE, HEAD_DIM), BF16)] * X,
        in_specs=[pl.BlockSpec(memory_space=pltpu.SMEM), vm, vm],
        out_specs=[vm] * X,
        compiler_params=PARAMS,
        name="merge_cores",
    )(ours, own, got)


def combine_kernel(x_ref, *refs):
    parts, (local_ref, stat_ref, out_ref, weight_ref) = refs[:X], refs[X:]
    parts = [parts[TURNS.index(s)] for s in range(X)]
    wide = HELD * ROWS
    lane_head = iota((LOCAL, HEAD_DIM), 1) // ROWS
    heads = [lax.rem(x_ref[0] + (X - s), X) * HELD for s in range(X)]
    log_total = jnp.zeros((LOCAL, HEAD_DIM), F32)
    for s in range(X):
        pieces = parts[s][LOCAL * wide :, :].astype(F32)
        lines = pieces + pltpu.roll(pieces, HEAD_DIM - ROWS, 1)
        lines = lines + pltpu.roll(pieces, HEAD_DIM - 2 * ROWS, 1)
        for h in range(HELD):
            head = heads[s] + h
            line = pltpu.roll(lines[h * LOCAL : (h + 1) * LOCAL], head * ROWS, 1)
            log_total = jnp.where(lane_head == head, line, log_total)
    local_max = stat_ref[:LOCAL, :]
    highest = jnp.maximum(log_total, local_max)
    prefix_part = jnp.exp(log_total - highest)
    local_part = jnp.exp(local_max - highest)
    whole = prefix_part + local_part * stat_ref[LOCAL:, :]
    blank = jnp.zeros((HEAD_DIM - 2 * LOCAL, HEAD_DIM), F32)
    weight_ref[...] = jnp.concatenate([prefix_part / whole, local_part / whole, blank], axis=0).T
    for s in range(X):
        rows = pl.ds(pl.multiple_of(heads[s] * ROWS, wide), wide)
        weights = weight_ref[rows, :]
        for r in range(LOCAL):
            prefix = parts[s][r * wide : (r + 1) * wide, :].astype(F32)
            out = weights[:, r : r + 1] * prefix
            out = out + weights[:, LOCAL + r : LOCAL + r + 1] * local_ref[r, rows, :]
            out_ref[r, rows, :] = out.astype(BF16)


def combine(x, parts, local_out, stats):
    vm = pl.BlockSpec(memory_space=pltpu.VMEM)
    return pl.pallas_call(
        combine_kernel,
        out_shape=jax.ShapeDtypeStruct((LOCAL, HEADS * STEPS, HEAD_DIM), BF16),
        in_specs=[pl.BlockSpec(memory_space=pltpu.SMEM)] + [vm] * (X + 2),
        out_specs=vm,
        scratch_shapes=[pltpu.VMEM((HEAD_DIM, HEAD_DIM), F32)],
        compiler_params=PARAMS,
        name="combine_parts",
    )(x, *parts, local_out, stats)


def turn_x(value, turns):
    return lax.ppermute(value, "x", [(i, (i + turns) % X) for i in range(X)])


def shift(value, turns):
    return lax.ppermute(value, "y", [(i, (i + turns) % Y) for i in range(Y)])


def swap_cores(value):
    return lax.ppermute(value, "core", [(i, 1 - i) for i in range(CORES)])


def onward(value):
    pairs = []
    for z in range(Z):
        pairs.append((z * CORES, (z + 1) % Z * CORES))
        pairs.append((z * CORES + 1, (z - 1) % Z * CORES + 1))
    return lax.ppermute(value, ("z", "core"), pairs)


def per_device(
    queries,
    new_keys,
    new_values,
    suffix_keys,
    suffix_values,
    suffix_length,
    group_ids,
    prefix_keys,
    prefix_values,
    prefix_length,
):
    z = lax.axis_index("z")
    core = lax.axis_index("core")
    x = lax.axis_index("x")
    at_x = x.reshape(1).astype(jnp.int32)

    def head_rows(value):
        heads = value.shape[2] // HEAD_DIM
        value = value.reshape(LOCAL, STEPS, heads, HEAD_DIM).transpose(0, 2, 1, 3)
        return value.reshape(LOCAL, heads * STEPS, HEAD_DIM)

    splits = split(at_x, head_rows(queries))
    mine = build_cache(prefix_length, prefix_keys, prefix_values, splits[0])
    arrived = [splits[0]] + [turn_x(splits[s], s) for s in range(1, X)]
    own_queries = stack([arrived[s] for s in TURNS])

    block_ids = group_ids[:, 0]
    ids = jnp.stack([block_ids, swap_cores(block_ids)])
    ids = lax.dynamic_slice_in_dim(
        jnp.concatenate([ids, ids], axis=1), x * LOCAL, X * LOCAL, axis=1
    ).reshape(COLUMN)
    index = jnp.arange(COLUMN, dtype=jnp.int32)
    block = index // (X * LOCAL)
    same = jnp.logical_and(ids[:, None] == ids[None, :], block[:, None] == block[None, :])
    position = jnp.sum(
        jnp.logical_and(same, index[:, None] > index[None, :]), axis=1, dtype=jnp.int32
    )
    turn = ((ids // CORES) % Y - lax.axis_index("y") + Y) % Y
    turn = jnp.where(turn < 2, turn, Y + 1 - turn)
    owner_core = ids % CORES
    ahead = (ids // (CORES * Y) - z + Z) % Z
    half = Z // 2
    side = jnp.where(ahead % half == 0, owner_core, (ahead < half).astype(jnp.int32))
    steps = jnp.where(ahead > half, Z - ahead, ahead)
    arrival = jnp.where(steps == 0, 0, 2 * steps - (owner_core == side).astype(jnp.int32))
    slot = block * (PER_GROUP // CORES) + position
    unit = arrival * (HELD * PER_GROUP) + slot
    place = turn * (UNITS * PER_GROUP) + unit
    ours = side == core
    counts = (EARLY * HELD * PER_GROUP, (OWNED - EARLY) * HELD * PER_GROUP)
    late_line = Y * padded(counts[0]) + turn * padded(counts[1]) + unit - counts[0]
    line = jnp.where(arrival < EARLY, turn * padded(counts[0]) + unit, late_line)
    line = jnp.where(ours, line, -HELD * PER_GROUP).reshape(CORES * X, 1, LOCAL)
    line = line + jnp.arange(HELD, dtype=jnp.int32)[:, None] * PER_GROUP
    line = line.reshape(COLUMN * HELD, 1)

    own_1, other_0 = onward(mine), swap_cores(mine)
    other_queries = swap_cores(own_queries)
    own_2, other_1 = onward(own_1), onward(other_0)
    packed = pack(jnp.where(ours, place, DUMP), own_queries, other_queries)
    received = [packed[0]] + [shift(packed[s], TURNS[s]) for s in range(1, Y)]
    own_3, other_2 = onward(own_2), onward(other_1)
    early = attend_prefix(0, received, [mine, own_1, other_1, own_2, other_2])
    own_4, other_3 = onward(own_3), onward(other_2)
    late = attend_prefix(EARLY, received, [own_3, other_3, own_4])
    parts = []
    for results in (early, late):
        parts += [results[0]] + [shift(results[s], -TURNS[s]) for s in range(1, Y)]

    local_out, stats = attend_local(
        suffix_length,
        head_rows(queries),
        suffix_keys,
        suffix_values,
        head_rows(new_keys),
        head_rows(new_values),
    )
    own_back, other_back = unpack(jnp.where(ours, place, 0), line, parts)
    pieces = merge(ours.astype(jnp.int32), own_back, swap_cores(other_back))
    got = [pieces[0]] + [turn_x(pieces[s], s) for s in range(1, X)]
    out = combine(at_x, [got[s] for s in TURNS], local_out, stats)
    out = out.reshape(LOCAL, HEADS, STEPS, HEAD_DIM).transpose(0, 2, 1, 3)
    return out.reshape(LOCAL, STEPS, HEADS * HEAD_DIM)


def solution(mesh):
    axes = ("z", "y", "core", "x")
    fine = Mesh(mesh.devices.reshape(Z, Y, CORES, X), axes)
    rows = P(axes, None, None)
    groups = ("z", "y", "core")
    placed = (rows,) * 5 + (
        P(axes),
        P(groups, None),
        P(groups, None, "x"),
        P(groups, None, "x"),
        P(groups),
    )
    return jax.shard_map(
        per_device, mesh=fine, in_specs=placed, out_specs=rows, check_vma=False
    )
```

```python
import functools
import math

import jax
import jax.numpy as jnp
from jax import lax
from jax.experimental import pallas as pl
from jax.experimental.pallas import tpu as pltpu
from jax.sharding import Mesh, PartitionSpec as P

HEADS = 64
KV_HEADS = 8
HEAD_DIM = 128
PREFIX_MAX = 256
STEPS = 2
SUFFIX_MAX = 32
GROUP = HEADS // KV_HEADS
ROWS = GROUP * STEPS
FACTOR = 1.0 / math.sqrt(HEAD_DIM)
Z, Y, CORES, X = 8, 4, 2, 4
PEERS = CORES * X
LOCAL = 8
COLUMN = PEERS * LOCAL
HELD = KV_HEADS // X
OWNED = Z
EARLY = 5
PER_GROUP = 4
BLOCK = PER_GROUP * ROWS
UNITS = OWNED * HELD
OUT_ROWS = UNITS * BLOCK
DUMP = Y * OUT_ROWS // ROWS
CACHE_ROWS = 2 * HELD * PREFIX_MAX
F32 = jnp.float32
BF16 = jnp.bfloat16
TURNS = (0, 1, 3, 2)
PARAMS = pltpu.CompilerParams(vmem_limit_bytes=32 * 1024 * 1024)


def padded(count):
    return -(-count // 16) * 16


def dot_t(a, b):
    return lax.dot_general(a, b, (((1,), (1,)), ((), ())), preferred_element_type=F32)


def iota(shape, dim):
    return lax.broadcasted_iota(jnp.int32, shape, dim)


def local_kernel(length_ref, q_ref, sk_ref, sv_ref, nk_ref, nv_ref, out_ref, stat_ref):
    width = KV_HEADS * SUFFIX_MAX
    fresh = KV_HEADS * STEPS
    row = iota((HEADS * STEPS, width), 0)
    col = iota((HEADS * STEPS, width), 1)
    same_head = row // ROWS == col // SUFFIX_MAX
    position = col % SUFFIX_MAX
    row2 = iota((HEADS * STEPS, fresh), 0)
    col2 = iota((HEADS * STEPS, fresh), 1)
    seen = jnp.logical_and(row2 // ROWS == col2 // STEPS, col2 % STEPS <= row2 % STEPS)
    lane = iota((HEADS * STEPS, HEAD_DIM), 1)
    columns = jnp.zeros((HEADS * STEPS, HEAD_DIM), F32)
    for r in range(LOCAL):
        q = q_ref[r]
        keys = jnp.concatenate(
            [sk_ref[r, :, k * HEAD_DIM : (k + 1) * HEAD_DIM] for k in range(KV_HEADS)], axis=0
        )
        values = jnp.concatenate(
            [sv_ref[r, :, k * HEAD_DIM : (k + 1) * HEAD_DIM] for k in range(KV_HEADS)], axis=0
        )
        usable = jnp.logical_and(same_head, position < length_ref[r])
        old = jnp.where(usable, dot_t(q, keys) * FACTOR, -jnp.inf)
        new = jnp.where(seen, dot_t(q, nk_ref[r]) * FACTOR, -jnp.inf)
        highest = jnp.maximum(
            jnp.max(old, axis=1, keepdims=True), jnp.max(new, axis=1, keepdims=True)
        )
        old = jnp.exp(old - highest)
        new = jnp.exp(new - highest)
        total = jnp.sum(old, axis=1, keepdims=True) + jnp.sum(new, axis=1, keepdims=True)
        out = jnp.dot(old.astype(BF16), values, preferred_element_type=F32)
        out_ref[r] = out + jnp.dot(new.astype(BF16), nv_ref[r], preferred_element_type=F32)
        columns = jnp.where(lane == r, highest, jnp.where(lane == LOCAL + r, total, columns))
    stat_ref[...] = columns.T[: 2 * LOCAL]


def attend_local(lengths, q, sk, sv, nk, nv):
    vm = pl.BlockSpec(memory_space=pltpu.VMEM)
    shape = jax.ShapeDtypeStruct((LOCAL, HEADS * STEPS, HEAD_DIM), F32)
    return pl.pallas_call(
        local_kernel,
        out_shape=(shape, jax.ShapeDtypeStruct((2 * LOCAL, HEADS * STEPS), F32)),
        in_specs=[pl.BlockSpec(memory_space=pltpu.SMEM)] + [vm] * 5,
        out_specs=(vm, vm),
        compiler_params=PARAMS,
        name="local_attention",
    )(lengths, q, sk, sv, nk, nv)


def split_kernel(x_ref, q_ref, *refs):
    out_refs, sems = refs[:X], refs[X]
    wide = HELD * ROWS
    copies = []
    for s in range(X):
        head = pl.multiple_of(lax.rem(x_ref[0] + s, X) * wide, wide)
        for r in range(LOCAL):
            copies.append(
                pltpu.make_async_copy(
                    q_ref.at[r, pl.ds(head, wide), :],
                    out_refs[s].at[pl.ds(r * wide, wide), :],
                    sems.at[s, r],
                )
            )
    for copy in copies:
        copy.start()
    for copy in copies:
        copy.wait()


def split(x, q):
    part = jax.ShapeDtypeStruct((LOCAL * HELD * ROWS, HEAD_DIM), BF16)
    return pl.pallas_call(
        split_kernel,
        out_shape=[part] * X,
        in_specs=[pl.BlockSpec(memory_space=pltpu.SMEM), pl.BlockSpec(memory_space=pl.ANY)],
        out_specs=[pl.BlockSpec(memory_space=pltpu.VMEM)] * X,
        scratch_shapes=[pltpu.SemaphoreType.DMA((X, LOCAL))],
        compiler_params=PARAMS,
        name="split_queries",
    )(x, q)


def cache_kernel(length_ref, k_ref, v_ref, after_ref, cache_ref, sems):
    copies = []
    for i, ref in enumerate((k_ref, v_ref)):
        for h in range(HELD):
            at = (i * HELD + h) * PREFIX_MAX
            copies.append(
                pltpu.make_async_copy(
                    ref.at[0, :, pl.ds(h * HEAD_DIM, HEAD_DIM)],
                    cache_ref.at[pl.ds(at, PREFIX_MAX), :],
                    sems.at[i, h],
                )
            )
    for copy in copies:
        copy.start()
    length = jnp.full((16, HEAD_DIM), length_ref[0], jnp.int32)
    cache_ref[CACHE_ROWS:, :] = length.astype(F32).astype(BF16)
    for copy in copies:
        copy.wait()


def build_cache(length, keys, values, after):
    anywhere = pl.BlockSpec(memory_space=pl.ANY)
    return pl.pallas_call(
        cache_kernel,
        out_shape=jax.ShapeDtypeStruct((CACHE_ROWS + 16, HEAD_DIM), BF16),
        in_specs=[pl.BlockSpec(memory_space=pltpu.SMEM)] + [anywhere] * 3,
        out_specs=pl.BlockSpec(memory_space=pltpu.VMEM),
        scratch_shapes=[pltpu.SemaphoreType.DMA((2, HELD))],
        compiler_params=PARAMS,
        name="build_cache",
    )(length, keys, values, after)


def stack_kernel(*refs):
    parts, out_ref = refs[:-1], refs[-1]
    size = parts[0].shape[0]
    for i, ref in enumerate(parts):
        out_ref[i * size : (i + 1) * size, :] = ref[...]


def stack(parts):
    vm = pl.BlockSpec(memory_space=pltpu.VMEM)
    size, width = parts[0].shape
    return pl.pallas_call(
        stack_kernel,
        out_shape=jax.ShapeDtypeStruct((len(parts) * size, width), parts[0].dtype),
        in_specs=[vm] * len(parts),
        out_specs=vm,
        compiler_params=PARAMS,
        name="stack_queries",
    )(*parts)


def pack_kernel(place_ref, own_ref, other_ref, *out_refs):
    packed_ref = out_refs[Y]
    packed_ref[...] = jnp.zeros(packed_ref.shape, BF16)
    half = COLUMN // CORES
    for i in range(COLUMN):
        q_ref = own_ref if i < half else other_ref
        for h in range(HELD):
            start = pl.multiple_of((place_ref[i] + h * PER_GROUP) * ROWS, ROWS)
            at = ((i % half) * HELD + h) * ROWS
            packed_ref[pl.ds(start, ROWS), :] = q_ref[at : at + ROWS, :]
    for s in range(Y):
        out_refs[s][...] = packed_ref[s * OUT_ROWS : (s + 1) * OUT_ROWS, :]


def pack(place, own, other):
    vm = pl.BlockSpec(memory_space=pltpu.VMEM)
    return pl.pallas_call(
        pack_kernel,
        out_shape=[jax.ShapeDtypeStruct((OUT_ROWS, HEAD_DIM), BF16)] * Y,
        in_specs=[pl.BlockSpec(memory_space=pltpu.SMEM), vm, vm],
        out_specs=[vm] * Y,
        scratch_shapes=[pltpu.VMEM((Y * OUT_ROWS + 2 * BLOCK, HEAD_DIM), BF16)],
        compiler_params=PARAMS,
        name="pack_queries",
    )(place, own, other)


def prefix_kernel(first, count, *refs):
    q_refs, caches, out_refs = refs[:Y], refs[Y : Y + count], refs[Y + count :]
    column = iota((1, PREFIX_MAX), 1).astype(F32)
    lane = iota((Y * BLOCK, HEAD_DIM), 1)
    diagonal = lane % ROWS == iota((Y * BLOCK, HEAD_DIM), 0) % ROWS
    piece = iota((Y * PER_GROUP, HEAD_DIM), 1) // ROWS
    lines = []
    for j in range(count):
        length = caches[j][CACHE_ROWS:, :].astype(F32)[:1, :1]
        usable = column < length
        for h in range(HELD):
            unit = (first + j) * HELD + h
            q = jnp.concatenate(
                [ref[unit * BLOCK : (unit + 1) * BLOCK, :] for ref in q_refs], axis=0
            )
            keys = caches[j][h * PREFIX_MAX : (h + 1) * PREFIX_MAX, :]
            values = caches[j][(HELD + h) * PREFIX_MAX : (HELD + h + 1) * PREFIX_MAX, :]
            scores = jnp.where(usable, dot_t(q, keys) * FACTOR, -jnp.inf)
            highest = jnp.max(scores, axis=1, keepdims=True)
            weights = jnp.exp(scores - highest)
            total = jnp.sum(weights, axis=1, keepdims=True)
            out = jnp.dot(weights.astype(BF16), values, preferred_element_type=F32)
            out = (out / total).astype(BF16)
            at = (j * HELD + h) * BLOCK
            for s in range(Y):
                out_refs[s][at : at + BLOCK, :] = out[s * BLOCK : (s + 1) * BLOCK]
            log_total = jnp.where(diagonal, highest + jnp.log(total), 0.0)
            line = jnp.sum(log_total.reshape(Y * PER_GROUP, ROWS, HEAD_DIM), axis=1)
            upper = line.astype(BF16).astype(F32)
            remain = line - upper
            middle = remain.astype(BF16).astype(F32)
            lowest = remain - middle
            lines.append(jnp.where(piece == 0, upper, jnp.where(piece == 1, middle, lowest)))
    units = count * HELD
    blank = padded(units * PER_GROUP) - units * PER_GROUP
    for s in range(Y):
        part = [x[s * PER_GROUP : (s + 1) * PER_GROUP] for x in lines]
        if blank:
            part.append(jnp.zeros((blank, HEAD_DIM), F32))
        out_refs[s][units * BLOCK :, :] = jnp.concatenate(part, axis=0).astype(BF16)


def attend_prefix(first, queries, caches):
    count = len(caches)
    units = count * HELD
    rows = units * BLOCK + padded(units * PER_GROUP)
    vm = pl.BlockSpec(memory_space=pltpu.VMEM)
    return pl.pallas_call(
        functools.partial(prefix_kernel, first, count),
        out_shape=[jax.ShapeDtypeStruct((rows, HEAD_DIM), BF16)] * Y,
        in_specs=[vm] * (Y + count),
        out_specs=[vm] * Y,
        compiler_params=PARAMS,
        name="prefix_attention_%d" % first,
    )(*queries, *caches)


PIECE = LOCAL * HELD * (ROWS + 1)


def unpack_kernel(place_ref, line_ref, *refs):
    early, late = refs[:Y], refs[Y : 2 * Y]
    own_ref, other_ref, all_ref = refs[2 * Y :]
    for s in range(Y):
        base = s * OUT_ROWS
        cut = EARLY * HELD * BLOCK
        all_ref[base : base + cut, :] = early[s][:cut, :]
        all_ref[base + cut : base + OUT_ROWS, :] = late[s][: OUT_ROWS - cut, :]
    sources = jnp.concatenate(
        [ref[EARLY * HELD * BLOCK :, :] for ref in early]
        + [ref[(OWNED - EARLY) * HELD * BLOCK :, :] for ref in late],
        axis=0,
    )
    half = COLUMN // CORES
    size = LOCAL * HELD
    for i in range(COLUMN):
        out_ref = own_ref if i < half else other_ref
        base = (i % half) // LOCAL * PIECE
        for h in range(HELD):
            rows = pl.ds(pl.multiple_of((place_ref[i] + h * PER_GROUP) * ROWS, ROWS), ROWS)
            at = base + ((i % LOCAL) * HELD + h) * ROWS
            out_ref[at : at + ROWS, :] = all_ref[rows, :]
    wanted = line_ref[...] == iota((COLUMN * HELD, sources.shape[0]), 1)
    lines = jnp.dot(wanted.astype(BF16), sources, preferred_element_type=F32).astype(BF16)
    for i, out_ref in enumerate((own_ref, other_ref)):
        for x in range(X):
            at = (i * X + x) * size
            out_ref[x * PIECE + size * ROWS : (x + 1) * PIECE, :] = lines[at : at + size]


def unpack(place, line, parts):
    vm = pl.BlockSpec(memory_space=pltpu.VMEM)
    return pl.pallas_call(
        unpack_kernel,
        out_shape=[jax.ShapeDtypeStruct((X * PIECE, HEAD_DIM), BF16)] * CORES,
        in_specs=[pl.BlockSpec(memory_space=pltpu.SMEM)] + [vm] * (1 + 2 * Y),
        out_specs=[vm] * CORES,
        scratch_shapes=[pltpu.VMEM((Y * OUT_ROWS, HEAD_DIM), BF16)],
        compiler_params=PARAMS,
        name="unpack_results",
    )(place, line, *parts)


def merge_kernel(ours_ref, own_ref, got_ref, *out_refs):
    wide = HELD * ROWS
    for x in range(X):
        for r in range(LOCAL):
            rows = slice(x * PIECE + r * wide, x * PIECE + (r + 1) * wide)
            mine = ours_ref[x * LOCAL + r] == 1
            out_refs[x][r * wide : (r + 1) * wide, :] = jnp.where(
                mine, own_ref[rows, :], got_ref[rows, :]
            )
        rows = slice(x * PIECE + LOCAL * wide, (x + 1) * PIECE)
        out_refs[x][LOCAL * wide :, :] = own_ref[rows, :] + got_ref[rows, :]


def merge(ours, own, got):
    vm = pl.BlockSpec(memory_space=pltpu.VMEM)
    return pl.pallas_call(
        merge_kernel,
        out_shape=[jax.ShapeDtypeStruct((PIECE, HEAD_DIM), BF16)] * X,
        in_specs=[pl.BlockSpec(memory_space=pltpu.SMEM), vm, vm],
        out_specs=[vm] * X,
        compiler_params=PARAMS,
        name="merge_cores",
    )(ours, own, got)


def combine_kernel(x_ref, *refs):
    parts, (local_ref, stat_ref, out_ref, weight_ref) = refs[:X], refs[X:]
    parts = [parts[TURNS.index(s)] for s in range(X)]
    wide = HELD * ROWS
    lane_head = iota((LOCAL, HEAD_DIM), 1) // ROWS
    heads = [lax.rem(x_ref[0] + (X - s), X) * HELD for s in range(X)]
    log_total = jnp.zeros((LOCAL, HEAD_DIM), F32)
    for s in range(X):
        pieces = parts[s][LOCAL * wide :, :].astype(F32)
        lines = pieces + pltpu.roll(pieces, HEAD_DIM - ROWS, 1)
        lines = lines + pltpu.roll(pieces, HEAD_DIM - 2 * ROWS, 1)
        for h in range(HELD):
            head = heads[s] + h
            line = pltpu.roll(lines[h * LOCAL : (h + 1) * LOCAL], head * ROWS, 1)
            log_total = jnp.where(lane_head == head, line, log_total)
    local_max = stat_ref[:LOCAL, :]
    highest = jnp.maximum(log_total, local_max)
    prefix_part = jnp.exp(log_total - highest)
    local_part = jnp.exp(local_max - highest)
    whole = prefix_part + local_part * stat_ref[LOCAL:, :]
    blank = jnp.zeros((HEAD_DIM - 2 * LOCAL, HEAD_DIM), F32)
    weight_ref[...] = jnp.concatenate([prefix_part / whole, local_part / whole, blank], axis=0).T
    for s in range(X):
        rows = pl.ds(pl.multiple_of(heads[s] * ROWS, wide), wide)
        weights = weight_ref[rows, :]
        for r in range(LOCAL):
            prefix = parts[s][r * wide : (r + 1) * wide, :].astype(F32)
            out = weights[:, r : r + 1] * prefix
            out = out + weights[:, LOCAL + r : LOCAL + r + 1] * local_ref[r, rows, :]
            out_ref[r, rows, :] = out.astype(BF16)


def combine(x, parts, local_out, stats):
    vm = pl.BlockSpec(memory_space=pltpu.VMEM)
    return pl.pallas_call(
        combine_kernel,
        out_shape=jax.ShapeDtypeStruct((LOCAL, HEADS * STEPS, HEAD_DIM), BF16),
        in_specs=[pl.BlockSpec(memory_space=pltpu.SMEM)] + [vm] * (X + 2),
        out_specs=vm,
        scratch_shapes=[pltpu.VMEM((HEAD_DIM, HEAD_DIM), F32)],
        compiler_params=PARAMS,
        name="combine_parts",
    )(x, *parts, local_out, stats)


def turn_x(value, turns):
    return lax.ppermute(value, "x", [(i, (i + turns) % X) for i in range(X)])


def shift(value, turns):
    return lax.ppermute(value, "y", [(i, (i + turns) % Y) for i in range(Y)])


def swap_cores(value):
    return lax.ppermute(value, "core", [(i, 1 - i) for i in range(CORES)])


def onward(value):
    pairs = []
    for z in range(Z):
        pairs.append((z * CORES, (z + 1) % Z * CORES))
        pairs.append((z * CORES + 1, (z - 1) % Z * CORES + 1))
    return lax.ppermute(value, ("z", "core"), pairs)


def per_device(
    queries,
    new_keys,
    new_values,
    suffix_keys,
    suffix_values,
    suffix_length,
    group_ids,
    prefix_keys,
    prefix_values,
    prefix_length,
):
    z = lax.axis_index("z")
    core = lax.axis_index("core")
    x = lax.axis_index("x")
    at_x = x.reshape(1).astype(jnp.int32)

    def head_rows(value):
        heads = value.shape[2] // HEAD_DIM
        value = value.reshape(LOCAL, STEPS, heads, HEAD_DIM).transpose(0, 2, 1, 3)
        return value.reshape(LOCAL, heads * STEPS, HEAD_DIM)

    splits = split(at_x, head_rows(queries))
    mine = build_cache(prefix_length, prefix_keys, prefix_values, splits[0])
    arrived = [splits[0]] + [turn_x(splits[s], s) for s in range(1, X)]
    own_queries = stack([arrived[-s % X] for s in range(X)])

    block_ids = group_ids[:, 0]
    ids = jnp.stack([block_ids, swap_cores(block_ids)])
    ids = lax.dynamic_slice_in_dim(
        jnp.concatenate([ids, ids], axis=1), x * LOCAL, X * LOCAL, axis=1
    ).reshape(COLUMN)
    index = jnp.arange(COLUMN, dtype=jnp.int32)
    block = index // (X * LOCAL)
    same = jnp.logical_and(ids[:, None] == ids[None, :], block[:, None] == block[None, :])
    position = jnp.sum(
        jnp.logical_and(same, index[:, None] > index[None, :]), axis=1, dtype=jnp.int32
    )
    turn = ((ids // CORES) % Y - lax.axis_index("y") + Y) % Y
    turn = jnp.where(turn < 2, turn, Y + 1 - turn)
    owner_core = ids % CORES
    ahead = (ids // (CORES * Y) - z + Z) % Z
    half = Z // 2
    side = jnp.where(ahead % half == 0, owner_core, (ahead < half).astype(jnp.int32))
    steps = jnp.where(ahead > half, Z - ahead, ahead)
    arrival = jnp.where(steps == 0, 0, 2 * steps - (owner_core == side).astype(jnp.int32))
    slot = block * (PER_GROUP // CORES) + position
    unit = arrival * (HELD * PER_GROUP) + slot
    place = turn * (UNITS * PER_GROUP) + unit
    ours = side == core
    counts = (EARLY * HELD * PER_GROUP, (OWNED - EARLY) * HELD * PER_GROUP)
    late_line = Y * padded(counts[0]) + turn * padded(counts[1]) + unit - counts[0]
    line = jnp.where(arrival < EARLY, turn * padded(counts[0]) + unit, late_line)
    line = jnp.where(ours, line, -HELD * PER_GROUP).reshape(CORES * X, 1, LOCAL)
    line = line + jnp.arange(HELD, dtype=jnp.int32)[:, None] * PER_GROUP
    line = line.reshape(COLUMN * HELD, 1)

    own_1, other_0 = onward(mine), swap_cores(mine)
    other_queries = swap_cores(own_queries)
    own_2, other_1 = onward(own_1), onward(other_0)
    packed = pack(jnp.where(ours, place, DUMP), own_queries, other_queries)
    received = [packed[0]] + [shift(packed[s], TURNS[s]) for s in range(1, Y)]
    own_3, other_2 = onward(own_2), onward(other_1)
    early = attend_prefix(0, received, [mine, own_1, other_1, own_2, other_2])
    own_4, other_3 = onward(own_3), onward(other_2)
    late = attend_prefix(EARLY, received, [own_3, other_3, own_4])
    parts = []
    for results in (early, late):
        parts += [results[0]] + [shift(results[s], -TURNS[s]) for s in range(1, Y)]

    local_queries, parts[Y] = lax.optimization_barrier((head_rows(queries), parts[Y]))
    local_out, stats = attend_local(
        suffix_length,
        local_queries,
        suffix_keys,
        suffix_values,
        head_rows(new_keys),
        head_rows(new_values),
    )
    *parts, local_out, stats = lax.optimization_barrier((*parts, local_out, stats))
    own_back, other_back = unpack(jnp.where(ours, place, 0), line, parts)
    pieces = merge(ours.astype(jnp.int32), own_back, swap_cores(other_back))
    got = [pieces[0]] + [turn_x(pieces[s], s) for s in range(1, X)]
    out = combine(at_x, [got[s] for s in TURNS], local_out, stats)
    out = out.reshape(LOCAL, HEADS, STEPS, HEAD_DIM).transpose(0, 2, 1, 3)
    return out.reshape(LOCAL, STEPS, HEADS * HEAD_DIM)


def solution(mesh):
    axes = ("z", "y", "core", "x")
    fine = Mesh(mesh.devices.reshape(Z, Y, CORES, X), axes)
    rows = P(axes, None, None)
    groups = ("z", "y", "core")
    placed = (rows,) * 5 + (
        P(axes),
        P(groups, None),
        P(groups, None, "x"),
        P(groups, None, "x"),
        P(groups),
    )
    return jax.shard_map(
        per_device, mesh=fine, in_specs=placed, out_specs=rows, check_vma=False
    )
```

```python
import functools
import math

import jax
import jax.numpy as jnp
from jax import lax
from jax.experimental import pallas as pl
from jax.experimental.pallas import tpu as pltpu
from jax.sharding import Mesh, PartitionSpec as P

HEADS = 64
KV_HEADS = 8
HEAD_DIM = 128
PREFIX_MAX = 256
STEPS = 2
SUFFIX_MAX = 32
GROUP = HEADS // KV_HEADS
ROWS = GROUP * STEPS
FACTOR = 1.0 / math.sqrt(HEAD_DIM)
Z, Y, CORES, X = 8, 4, 2, 4
PEERS = CORES * X
LOCAL = 8
COLUMN = PEERS * LOCAL
HELD = KV_HEADS // X
OWNED = Z
EARLY = 4
PER_GROUP = 4
BLOCK = PER_GROUP * ROWS
UNITS = OWNED * HELD
OUT_ROWS = UNITS * BLOCK
DUMP = Y * OUT_ROWS // ROWS
CACHE_ROWS = 2 * HELD * PREFIX_MAX
F32 = jnp.float32
BF16 = jnp.bfloat16
TURNS = (0, 1, 3, 2)
PARAMS = pltpu.CompilerParams(vmem_limit_bytes=32 * 1024 * 1024)


def padded(count):
    return -(-count // 16) * 16


def dot_t(a, b):
    return lax.dot_general(a, b, (((1,), (1,)), ((), ())), preferred_element_type=F32)


def iota(shape, dim):
    return lax.broadcasted_iota(jnp.int32, shape, dim)


def local_kernel(length_ref, q_ref, sk_ref, sv_ref, nk_ref, nv_ref, out_ref, stat_ref):
    width = KV_HEADS * SUFFIX_MAX
    fresh = KV_HEADS * STEPS
    row = iota((HEADS * STEPS, width), 0)
    col = iota((HEADS * STEPS, width), 1)
    same_head = row // ROWS == col // SUFFIX_MAX
    position = col % SUFFIX_MAX
    row2 = iota((HEADS * STEPS, fresh), 0)
    col2 = iota((HEADS * STEPS, fresh), 1)
    seen = jnp.logical_and(row2 // ROWS == col2 // STEPS, col2 % STEPS <= row2 % STEPS)
    lane = iota((HEADS * STEPS, HEAD_DIM), 1)
    columns = jnp.zeros((HEADS * STEPS, HEAD_DIM), F32)
    for r in range(LOCAL):
        q = q_ref[r]
        keys = jnp.concatenate(
            [sk_ref[r, :, k * HEAD_DIM : (k + 1) * HEAD_DIM] for k in range(KV_HEADS)], axis=0
        )
        values = jnp.concatenate(
            [sv_ref[r, :, k * HEAD_DIM : (k + 1) * HEAD_DIM] for k in range(KV_HEADS)], axis=0
        )
        usable = jnp.logical_and(same_head, position < length_ref[r])
        old = jnp.where(usable, dot_t(q, keys) * FACTOR, -jnp.inf)
        new = jnp.where(seen, dot_t(q, nk_ref[r]) * FACTOR, -jnp.inf)
        highest = jnp.maximum(
            jnp.max(old, axis=1, keepdims=True), jnp.max(new, axis=1, keepdims=True)
        )
        old = jnp.exp(old - highest)
        new = jnp.exp(new - highest)
        total = jnp.sum(old, axis=1, keepdims=True) + jnp.sum(new, axis=1, keepdims=True)
        out = jnp.dot(old.astype(BF16), values, preferred_element_type=F32)
        out_ref[r] = out + jnp.dot(new.astype(BF16), nv_ref[r], preferred_element_type=F32)
        columns = jnp.where(lane == r, highest, jnp.where(lane == LOCAL + r, total, columns))
    stat_ref[...] = columns.T[: 2 * LOCAL]


def attend_local(lengths, q, sk, sv, nk, nv):
    vm = pl.BlockSpec(memory_space=pltpu.VMEM)
    shape = jax.ShapeDtypeStruct((LOCAL, HEADS * STEPS, HEAD_DIM), F32)
    return pl.pallas_call(
        local_kernel,
        out_shape=(shape, jax.ShapeDtypeStruct((2 * LOCAL, HEADS * STEPS), F32)),
        in_specs=[pl.BlockSpec(memory_space=pltpu.SMEM)] + [vm] * 5,
        out_specs=(vm, vm),
        compiler_params=PARAMS,
        name="local_attention",
    )(lengths, q, sk, sv, nk, nv)


def split_kernel(x_ref, q_ref, *refs):
    out_refs, sems = refs[:X], refs[X]
    wide = HELD * ROWS
    copies = []
    for s in range(X):
        head = pl.multiple_of(lax.rem(x_ref[0] + s, X) * wide, wide)
        for r in range(LOCAL):
            copies.append(
                pltpu.make_async_copy(
                    q_ref.at[r, pl.ds(head, wide), :],
                    out_refs[s].at[pl.ds(r * wide, wide), :],
                    sems.at[s, r],
                )
            )
    for copy in copies:
        copy.start()
    for copy in copies:
        copy.wait()


def split(x, q):
    part = jax.ShapeDtypeStruct((LOCAL * HELD * ROWS, HEAD_DIM), BF16)
    return pl.pallas_call(
        split_kernel,
        out_shape=[part] * X,
        in_specs=[pl.BlockSpec(memory_space=pltpu.SMEM), pl.BlockSpec(memory_space=pl.ANY)],
        out_specs=[pl.BlockSpec(memory_space=pltpu.VMEM)] * X,
        scratch_shapes=[pltpu.SemaphoreType.DMA((X, LOCAL))],
        compiler_params=PARAMS,
        name="split_queries",
    )(x, q)


def cache_kernel(length_ref, k_ref, v_ref, after_ref, cache_ref, sems):
    copies = []
    for i, ref in enumerate((k_ref, v_ref)):
        for h in range(HELD):
            at = (i * HELD + h) * PREFIX_MAX
            copies.append(
                pltpu.make_async_copy(
                    ref.at[0, :, pl.ds(h * HEAD_DIM, HEAD_DIM)],
                    cache_ref.at[pl.ds(at, PREFIX_MAX), :],
                    sems.at[i, h],
                )
            )
    for copy in copies:
        copy.start()
    length = jnp.full((16, HEAD_DIM), length_ref[0], jnp.int32)
    cache_ref[CACHE_ROWS:, :] = length.astype(F32).astype(BF16)
    for copy in copies:
        copy.wait()


def build_cache(length, keys, values, after):
    anywhere = pl.BlockSpec(memory_space=pl.ANY)
    return pl.pallas_call(
        cache_kernel,
        out_shape=jax.ShapeDtypeStruct((CACHE_ROWS + 16, HEAD_DIM), BF16),
        in_specs=[pl.BlockSpec(memory_space=pltpu.SMEM)] + [anywhere] * 3,
        out_specs=pl.BlockSpec(memory_space=pltpu.VMEM),
        scratch_shapes=[pltpu.SemaphoreType.DMA((2, HELD))],
        compiler_params=PARAMS,
        name="build_cache",
    )(length, keys, values, after)


def stack_kernel(*refs):
    parts, out_ref = refs[:-1], refs[-1]
    size = parts[0].shape[0]
    for i, ref in enumerate(parts):
        out_ref[i * size : (i + 1) * size, :] = ref[...]


def stack(parts):
    vm = pl.BlockSpec(memory_space=pltpu.VMEM)
    size, width = parts[0].shape
    return pl.pallas_call(
        stack_kernel,
        out_shape=jax.ShapeDtypeStruct((len(parts) * size, width), parts[0].dtype),
        in_specs=[vm] * len(parts),
        out_specs=vm,
        compiler_params=PARAMS,
        name="stack_queries",
    )(*parts)


def pack_kernel(place_ref, own_ref, other_ref, *out_refs):
    packed_ref = out_refs[Y]
    packed_ref[...] = jnp.zeros(packed_ref.shape, BF16)
    half = COLUMN // CORES
    for i in range(COLUMN):
        q_ref = own_ref if i < half else other_ref
        for h in range(HELD):
            start = pl.multiple_of((place_ref[i] + h * PER_GROUP) * ROWS, ROWS)
            at = ((i % half) * HELD + h) * ROWS
            packed_ref[pl.ds(start, ROWS), :] = q_ref[at : at + ROWS, :]
    for s in range(Y):
        out_refs[s][...] = packed_ref[s * OUT_ROWS : (s + 1) * OUT_ROWS, :]


def pack(place, own, other):
    vm = pl.BlockSpec(memory_space=pltpu.VMEM)
    return pl.pallas_call(
        pack_kernel,
        out_shape=[jax.ShapeDtypeStruct((OUT_ROWS, HEAD_DIM), BF16)] * Y,
        in_specs=[pl.BlockSpec(memory_space=pltpu.SMEM), vm, vm],
        out_specs=[vm] * Y,
        scratch_shapes=[pltpu.VMEM((Y * OUT_ROWS + 2 * BLOCK, HEAD_DIM), BF16)],
        compiler_params=PARAMS,
        name="pack_queries",
    )(place, own, other)


def prefix_kernel(first, count, *refs):
    q_refs, caches, out_refs = refs[:Y], refs[Y : Y + count], refs[Y + count :]
    column = iota((1, PREFIX_MAX), 1).astype(F32)
    lane = iota((Y * BLOCK, HEAD_DIM), 1)
    diagonal = lane % ROWS == iota((Y * BLOCK, HEAD_DIM), 0) % ROWS
    piece = iota((Y * PER_GROUP, HEAD_DIM), 1) // ROWS
    lines = []
    for j in range(count):
        length = caches[j][CACHE_ROWS:, :].astype(F32)[:1, :1]
        usable = column < length
        for h in range(HELD):
            unit = (first + j) * HELD + h
            q = jnp.concatenate(
                [ref[unit * BLOCK : (unit + 1) * BLOCK, :] for ref in q_refs], axis=0
            )
            keys = caches[j][h * PREFIX_MAX : (h + 1) * PREFIX_MAX, :]
            values = caches[j][(HELD + h) * PREFIX_MAX : (HELD + h + 1) * PREFIX_MAX, :]
            scores = jnp.where(usable, dot_t(q, keys) * FACTOR, -jnp.inf)
            highest = jnp.max(scores, axis=1, keepdims=True)
            weights = jnp.exp(scores - highest)
            total = jnp.sum(weights, axis=1, keepdims=True)
            out = jnp.dot(weights.astype(BF16), values, preferred_element_type=F32)
            out = (out / total).astype(BF16)
            at = (j * HELD + h) * BLOCK
            for s in range(Y):
                out_refs[s][at : at + BLOCK, :] = out[s * BLOCK : (s + 1) * BLOCK]
            log_total = jnp.where(diagonal, highest + jnp.log(total), 0.0)
            line = jnp.sum(log_total.reshape(Y * PER_GROUP, ROWS, HEAD_DIM), axis=1)
            upper = line.astype(BF16).astype(F32)
            remain = line - upper
            middle = remain.astype(BF16).astype(F32)
            lowest = remain - middle
            lines.append(jnp.where(piece == 0, upper, jnp.where(piece == 1, middle, lowest)))
    units = count * HELD
    blank = padded(units * PER_GROUP) - units * PER_GROUP
    for s in range(Y):
        part = [x[s * PER_GROUP : (s + 1) * PER_GROUP] for x in lines]
        if blank:
            part.append(jnp.zeros((blank, HEAD_DIM), F32))
        out_refs[s][units * BLOCK :, :] = jnp.concatenate(part, axis=0).astype(BF16)


def attend_prefix(first, queries, caches):
    count = len(caches)
    units = count * HELD
    rows = units * BLOCK + padded(units * PER_GROUP)
    vm = pl.BlockSpec(memory_space=pltpu.VMEM)
    return pl.pallas_call(
        functools.partial(prefix_kernel, first, count),
        out_shape=[jax.ShapeDtypeStruct((rows, HEAD_DIM), BF16)] * Y,
        in_specs=[vm] * (Y + count),
        out_specs=[vm] * Y,
        compiler_params=PARAMS,
        name="prefix_attention_%d" % first,
    )(*queries, *caches)


PIECE = LOCAL * HELD * (ROWS + 1)


def unpack_kernel(place_ref, line_ref, *refs):
    early, late = refs[:Y], refs[Y : 2 * Y]
    own_ref, other_ref, all_ref = refs[2 * Y :]
    for s in range(Y):
        base = s * OUT_ROWS
        cut = EARLY * HELD * BLOCK
        all_ref[base : base + cut, :] = early[s][:cut, :]
        all_ref[base + cut : base + OUT_ROWS, :] = late[s][: OUT_ROWS - cut, :]
    sources = jnp.concatenate(
        [ref[EARLY * HELD * BLOCK :, :] for ref in early]
        + [ref[(OWNED - EARLY) * HELD * BLOCK :, :] for ref in late],
        axis=0,
    )
    half = COLUMN // CORES
    size = LOCAL * HELD
    for i in range(COLUMN):
        out_ref = own_ref if i < half else other_ref
        base = (i % half) // LOCAL * PIECE
        for h in range(HELD):
            rows = pl.ds(pl.multiple_of((place_ref[i] + h * PER_GROUP) * ROWS, ROWS), ROWS)
            at = base + ((i % LOCAL) * HELD + h) * ROWS
            out_ref[at : at + ROWS, :] = all_ref[rows, :]
    wanted = line_ref[...] == iota((COLUMN * HELD, sources.shape[0]), 1)
    lines = jnp.dot(wanted.astype(BF16), sources, preferred_element_type=F32).astype(BF16)
    for i, out_ref in enumerate((own_ref, other_ref)):
        for x in range(X):
            at = (i * X + x) * size
            out_ref[x * PIECE + size * ROWS : (x + 1) * PIECE, :] = lines[at : at + size]


def unpack(place, line, parts):
    vm = pl.BlockSpec(memory_space=pltpu.VMEM)
    return pl.pallas_call(
        unpack_kernel,
        out_shape=[jax.ShapeDtypeStruct((X * PIECE, HEAD_DIM), BF16)] * CORES,
        in_specs=[pl.BlockSpec(memory_space=pltpu.SMEM)] + [vm] * (1 + 2 * Y),
        out_specs=[vm] * CORES,
        scratch_shapes=[pltpu.VMEM((Y * OUT_ROWS, HEAD_DIM), BF16)],
        compiler_params=PARAMS,
        name="unpack_results",
    )(place, line, *parts)


def merge_kernel(ours_ref, own_ref, got_ref, *out_refs):
    wide = HELD * ROWS
    for x in range(X):
        for r in range(LOCAL):
            rows = slice(x * PIECE + r * wide, x * PIECE + (r + 1) * wide)
            mine = ours_ref[x * LOCAL + r] == 1
            out_refs[x][r * wide : (r + 1) * wide, :] = jnp.where(
                mine, own_ref[rows, :], got_ref[rows, :]
            )
        rows = slice(x * PIECE + LOCAL * wide, (x + 1) * PIECE)
        out_refs[x][LOCAL * wide :, :] = own_ref[rows, :] + got_ref[rows, :]


def merge(ours, own, got):
    vm = pl.BlockSpec(memory_space=pltpu.VMEM)
    return pl.pallas_call(
        merge_kernel,
        out_shape=[jax.ShapeDtypeStruct((PIECE, HEAD_DIM), BF16)] * X,
        in_specs=[pl.BlockSpec(memory_space=pltpu.SMEM), vm, vm],
        out_specs=[vm] * X,
        compiler_params=PARAMS,
        name="merge_cores",
    )(ours, own, got)


def combine_kernel(x_ref, *refs):
    parts, (local_ref, stat_ref, out_ref, weight_ref) = refs[:X], refs[X:]
    parts = [parts[TURNS.index(s)] for s in range(X)]
    wide = HELD * ROWS
    lane_head = iota((LOCAL, HEAD_DIM), 1) // ROWS
    heads = [lax.rem(x_ref[0] + (X - s), X) * HELD for s in range(X)]
    log_total = jnp.zeros((LOCAL, HEAD_DIM), F32)
    for s in range(X):
        pieces = parts[s][LOCAL * wide :, :].astype(F32)
        lines = pieces + pltpu.roll(pieces, HEAD_DIM - ROWS, 1)
        lines = lines + pltpu.roll(pieces, HEAD_DIM - 2 * ROWS, 1)
        for h in range(HELD):
            head = heads[s] + h
            line = pltpu.roll(lines[h * LOCAL : (h + 1) * LOCAL], head * ROWS, 1)
            log_total = jnp.where(lane_head == head, line, log_total)
    local_max = stat_ref[:LOCAL, :]
    highest = jnp.maximum(log_total, local_max)
    prefix_part = jnp.exp(log_total - highest)
    local_part = jnp.exp(local_max - highest)
    whole = prefix_part + local_part * stat_ref[LOCAL:, :]
    blank = jnp.zeros((HEAD_DIM - 2 * LOCAL, HEAD_DIM), F32)
    weight_ref[...] = jnp.concatenate([prefix_part / whole, local_part / whole, blank], axis=0).T
    for s in range(X):
        rows = pl.ds(pl.multiple_of(heads[s] * ROWS, wide), wide)
        weights = weight_ref[rows, :]
        for r in range(LOCAL):
            prefix = parts[s][r * wide : (r + 1) * wide, :].astype(F32)
            out = weights[:, r : r + 1] * prefix
            out = out + weights[:, LOCAL + r : LOCAL + r + 1] * local_ref[r, rows, :]
            out_ref[r, rows, :] = out.astype(BF16)


def combine(x, parts, local_out, stats):
    vm = pl.BlockSpec(memory_space=pltpu.VMEM)
    return pl.pallas_call(
        combine_kernel,
        out_shape=jax.ShapeDtypeStruct((LOCAL, HEADS * STEPS, HEAD_DIM), BF16),
        in_specs=[pl.BlockSpec(memory_space=pltpu.SMEM)] + [vm] * (X + 2),
        out_specs=vm,
        scratch_shapes=[pltpu.VMEM((HEAD_DIM, HEAD_DIM), F32)],
        compiler_params=PARAMS,
        name="combine_parts",
    )(x, *parts, local_out, stats)


def turn_x(value, turns):
    return lax.ppermute(value, "x", [(i, (i + turns) % X) for i in range(X)])


def shift(value, turns):
    return lax.ppermute(value, "y", [(i, (i + turns) % Y) for i in range(Y)])


def swap_cores(value):
    return lax.ppermute(value, "core", [(i, 1 - i) for i in range(CORES)])


def onward(value):
    pairs = []
    for z in range(Z):
        pairs.append((z * CORES, (z + 1) % Z * CORES))
        pairs.append((z * CORES + 1, (z - 1) % Z * CORES + 1))
    return lax.ppermute(value, ("z", "core"), pairs)


def per_device(
    queries,
    new_keys,
    new_values,
    suffix_keys,
    suffix_values,
    suffix_length,
    group_ids,
    prefix_keys,
    prefix_values,
    prefix_length,
):
    z = lax.axis_index("z")
    core = lax.axis_index("core")
    x = lax.axis_index("x")
    at_x = x.reshape(1).astype(jnp.int32)

    def head_rows(value):
        heads = value.shape[2] // HEAD_DIM
        value = value.reshape(LOCAL, STEPS, heads, HEAD_DIM).transpose(0, 2, 1, 3)
        return value.reshape(LOCAL, heads * STEPS, HEAD_DIM)

    splits = split(at_x, head_rows(queries))
    mine = build_cache(prefix_length, prefix_keys, prefix_values, splits[0])
    arrived = [splits[0]] + [turn_x(splits[s], s) for s in range(1, X)]
    own_queries = stack([arrived[-s % X] for s in range(X)])

    block_ids = group_ids[:, 0]
    ids = jnp.stack([block_ids, swap_cores(block_ids)])
    ids = lax.dynamic_slice_in_dim(
        jnp.concatenate([ids, ids], axis=1), x * LOCAL, X * LOCAL, axis=1
    ).reshape(COLUMN)
    index = jnp.arange(COLUMN, dtype=jnp.int32)
    block = index // (X * LOCAL)
    same = jnp.logical_and(ids[:, None] == ids[None, :], block[:, None] == block[None, :])
    position = jnp.sum(
        jnp.logical_and(same, index[:, None] > index[None, :]), axis=1, dtype=jnp.int32
    )
    turn = ((ids // CORES) % Y - lax.axis_index("y") + Y) % Y
    turn = jnp.where(turn < 2, turn, Y + 1 - turn)
    owner_core = ids % CORES
    ahead = (ids // (CORES * Y) - z + Z) % Z
    half = Z // 2
    side = jnp.where(ahead % half == 0, owner_core, (ahead < half).astype(jnp.int32))
    steps = jnp.where(ahead > half, Z - ahead, ahead)
    arrival = jnp.where(steps == 0, 0, 2 * steps - (owner_core == side).astype(jnp.int32))
    slot = block * (PER_GROUP // CORES) + position
    unit = arrival * (HELD * PER_GROUP) + slot
    place = turn * (UNITS * PER_GROUP) + unit
    ours = side == core
    counts = (EARLY * HELD * PER_GROUP, (OWNED - EARLY) * HELD * PER_GROUP)
    late_line = Y * padded(counts[0]) + turn * padded(counts[1]) + unit - counts[0]
    line = jnp.where(arrival < EARLY, turn * padded(counts[0]) + unit, late_line)
    line = jnp.where(ours, line, -HELD * PER_GROUP).reshape(CORES * X, 1, LOCAL)
    line = line + jnp.arange(HELD, dtype=jnp.int32)[:, None] * PER_GROUP
    line = line.reshape(COLUMN * HELD, 1)

    own_1, other_0 = onward(mine), swap_cores(mine)
    other_queries = swap_cores(own_queries)
    own_2, other_1 = onward(own_1), onward(other_0)
    packed = pack(jnp.where(ours, place, DUMP), own_queries, other_queries)
    received = [packed[0]] + [shift(packed[s], TURNS[s]) for s in range(1, Y)]
    own_3, other_2 = onward(own_2), onward(other_1)
    early = attend_prefix(0, received, [mine, own_1, other_1, own_2])
    own_4, other_3 = onward(own_3), onward(other_2)
    late = attend_prefix(EARLY, received, [other_2, own_3, other_3, own_4])
    parts = []
    for results in (early, late):
        parts += [results[0]] + [shift(results[s], -TURNS[s]) for s in range(1, Y)]

    local_queries, parts[Y] = lax.optimization_barrier((head_rows(queries), parts[Y]))
    local_out, stats = attend_local(
        suffix_length,
        local_queries,
        suffix_keys,
        suffix_values,
        head_rows(new_keys),
        head_rows(new_values),
    )
    *parts, local_out, stats = lax.optimization_barrier((*parts, local_out, stats))
    own_back, other_back = unpack(jnp.where(ours, place, 0), line, parts)
    pieces = merge(ours.astype(jnp.int32), own_back, swap_cores(other_back))
    got = [pieces[0]] + [turn_x(pieces[s], s) for s in range(1, X)]
    out = combine(at_x, [got[s] for s in TURNS], local_out, stats)
    out = out.reshape(LOCAL, HEADS, STEPS, HEAD_DIM).transpose(0, 2, 1, 3)
    return out.reshape(LOCAL, STEPS, HEADS * HEAD_DIM)


def solution(mesh):
    axes = ("z", "y", "core", "x")
    fine = Mesh(mesh.devices.reshape(Z, Y, CORES, X), axes)
    rows = P(axes, None, None)
    groups = ("z", "y", "core")
    placed = (rows,) * 5 + (
        P(axes),
        P(groups, None),
        P(groups, None, "x"),
        P(groups, None, "x"),
        P(groups),
    )
    return jax.shard_map(
        per_device, mesh=fine, in_specs=placed, out_specs=rows, check_vma=False
    )
```
